512 devices in a mesh: dp: 32 (over y, x_hi, core), mp: 16 (over x_lo, z).
Axes of the slice: x: 4 (x_hi: 2, x_lo: 2; x = x_hi * 2 + x_lo), y: 8, z: 8, core: 2. Of those that a mesh axis runs over, the one named last changes fastest.
Arguments:
- activations: bfloat16 [4096, 3072], P('dp', 'mp'), may hold values from -45 to 45
- cotangent: bfloat16 [4096, 3072], P('dp', 'mp'), may hold values from -6 to 6
- ln_gain: bfloat16 [3072], P('mp'), may hold values from 0.099609375 to 1.8984375
- w_in: bfloat16 [3072, 8192], P('dp', 'mp'), may hold values from -1 to 1
- w_out: bfloat16 [4096, 3072], P('mp'), may hold values from -0.09375 to 0.09375
- q_gain: bfloat16 [16, 128], P('mp'), may hold values from 0.5 to 4
- k_gain: bfloat16 [16, 128], P('mp'), may hold values from 0.5 to 4
Outputs:
- grad_x: bfloat16 [4096, 3072], P('dp', 'mp')
- grad_w_in: bfloat16 [3072, 8192], P('dp', 'mp')
- grad_w_out: bfloat16 [4096, 3072], P('mp')
- grad_ln_gain: float32 [3072], P('mp')
- grad_q_gain: float32 [16, 128], P('mp')
- grad_k_gain: float32 [16, 128], P('mp')
The draws below stay inside these ranges and needn't reach their ends.
All inputs are finite; a program needn't handle non-finite values.
Results may differ from the reference program's by a relative error of at most 0.03.
Values may be sent and summed in bfloat16 or wider, within the bound.
A program may use at most 64 MiB of HBM per device.

```python
import jax
import jax.numpy as jnp
from jax import lax

D = 3072
HEAD_DIM = 128
HEADS_DEV = 1
PATCHES = 128
IMG_DEV = 1
TOK_DEV = 128
TOKENS = 4096
HEADS = 16
C_DEV = 512
C_IN = 8192
C_OUT_DEV = 256
C_OUT = 4096
N_DP = 32
N_MP = 16


def draw_activations(key, part):
    key = jax.random.fold_in(key, 11)
    key_sample, key_cols, key_rows = jax.random.split(key, 3)
    column = jnp.arange(D, dtype=jnp.float32) / D
    col_log = jax.random.uniform(key_cols, (1, D), jnp.float32, 0.0, 1.0) + 0.477 * column[None, :] - 0.75
    row_log = jax.random.uniform(key_rows, (TOKENS, 1), jnp.float32, -0.3, 0.3)
    sample = jax.random.truncated_normal(key_sample, -4.0, 4.0, (TOKENS, D), jnp.float32)
    return (sample * 10.0 ** (col_log + row_log)).astype(jnp.bfloat16)


def draw_w_in(key, part):
    key = jax.random.fold_in(key, 23)
    full_shape = (D, C_IN // C_DEV, C_DEV)
    sample = jax.random.truncated_normal(key, -4.0, 4.0, full_shape, jnp.float32)
    return (sample * D ** (-0.5)).reshape(D, C_IN).astype(jnp.bfloat16)


def draw_q_gain(key, part):
    key = jax.random.fold_in(key, 37)
    sample = jax.random.uniform(key, (HEADS, HEAD_DIM), jnp.float32, 0.5, 2.0)
    return sample.astype(jnp.bfloat16)


def draw_k_gain(key, part):
    key = jax.random.fold_in(key, 41)
    sample = jax.random.uniform(key, (HEADS, HEAD_DIM), jnp.float32, 0.5, 2.0)
    return sample.astype(jnp.bfloat16)


def block_scale(key, dims, shards, smallest, top_value):
    def one(dim, shards_of):
        steps = jax.random.uniform(jax.random.fold_in(jax.random.fold_in(key, 6), dim), (shards_of,), jnp.float32, smallest / len(shards), top_value / len(shards))
        return jnp.repeat(jnp.exp(steps), dims[dim] // shards_of).reshape((-1,) + (1,) * (len(dims) - dim - 1))

    factor_of = one(*shards[0])
    for cut in shards[1:]:
        factor_of = factor_of * one(*cut)
    return factor_of


def noise(own_key, extent, scale, reach, shards=(), kind=jnp.bfloat16):
    level = block_scale(own_key, extent, shards, -0.22, 0.18) if shards else 1.0
    entries = jax.random.normal(own_key, extent, jnp.float32) * scale * level
    return jnp.minimum(jnp.maximum(entries, -reach), reach).astype(kind)


def setup_inputs(seed: int = 0) -> dict:
    streams_of = jax.random.split(jax.random.key(seed), 8)
    return {
        "activations": draw_activations(jax.random.fold_in(streams_of[7], 71), 0),
        "cotangent": noise(streams_of[1], (TOKENS, D), 1.0, 6.0, ((0, 32), (1, 16))),
        "ln_gain": jnp.clip(1.0 + 0.18 * jax.random.normal(streams_of[2], (D,), jnp.float32), 0.099609375, 1.8984375).astype(jnp.bfloat16),
        "w_in": draw_w_in(jax.random.fold_in(streams_of[7], 71), 0),
        "w_out": noise(streams_of[4], (C_OUT, D), C_OUT ** -0.5, 0.09375, ((0, 16),)),
        "q_gain": draw_q_gain(jax.random.fold_in(streams_of[7], 71), 0),
        "k_gain": draw_k_gain(jax.random.fold_in(streams_of[7], 71), 0),
    }


epsilon = 1e-06

def normalize(values):
    row_mean = lax.optimization_barrier(jnp.mean(values, axis=-1, keepdims=True))
    centred = values - row_mean
    inv_std = lax.rsqrt(lax.optimization_barrier(jnp.mean(centred * centred, axis=-1, keepdims=True)) + epsilon)
    return (centred * inv_std, inv_std)

def norm_back(grad_hat, x_hat, inv_std):
    mean_grad = lax.optimization_barrier(jnp.mean(grad_hat, axis=-1, keepdims=True))
    mean_cross = lax.optimization_barrier(jnp.mean(grad_hat * x_hat, axis=-1, keepdims=True))
    return inv_std * (grad_hat - mean_grad - x_hat * mean_cross)

def gelu_pair(pre_act):
    normal_cdf = 0.5 * (1.0 + lax.erf(pre_act * 0.7071067811865476))
    normal_pdf = jnp.exp(-0.5 * pre_act * pre_act) * 0.3989422804014327
    return (pre_act * normal_cdf, normal_cdf + pre_act * normal_pdf)

def attend(q_raw, k_raw, v_raw, grad_out, q_gain, k_gain):
    scaling = q_raw.shape[-1] ** (-0.5)
    q_hat, q_inv = normalize(q_raw)
    k_hat, k_inv = normalize(k_raw)
    q_normed = (q_hat * q_gain.astype(jnp.float32)).astype(jnp.bfloat16)
    k_normed = (k_hat * k_gain.astype(jnp.float32)).astype(jnp.bfloat16)
    v_bf = v_raw.astype(jnp.bfloat16)
    scores = jnp.einsum('ipgd,iqgd->igpq', q_normed.astype(jnp.float32), k_normed.astype(jnp.float32)) * scaling
    attn_prob = jax.nn.softmax(scores, axis=-1)
    prob_bf = attn_prob.astype(jnp.bfloat16)
    out_bf = jnp.einsum('igpq,iqgd->ipgd', prob_bf.astype(jnp.float32), v_bf.astype(jnp.float32)).astype(jnp.bfloat16)
    grad_prob = jnp.einsum('ipgd,iqgd->igpq', grad_out.astype(jnp.float32), v_bf.astype(jnp.float32))
    grad_v = jnp.einsum('igpq,ipgd->iqgd', prob_bf.astype(jnp.float32), grad_out.astype(jnp.float32))
    grad_score = (attn_prob * (grad_prob - lax.optimization_barrier(jnp.sum(attn_prob * grad_prob, axis=-1, keepdims=True))) * scaling).astype(jnp.bfloat16)
    grad_qn = jnp.einsum('igpq,iqgd->ipgd', grad_score.astype(jnp.float32), k_normed.astype(jnp.float32))
    grad_kn = jnp.einsum('igpq,ipgd->iqgd', grad_score.astype(jnp.float32), q_normed.astype(jnp.float32))
    q_gain_grad = lax.optimization_barrier(jnp.sum(grad_qn * q_hat, axis=(0, 1)))
    k_gain_grad = lax.optimization_barrier(jnp.sum(grad_kn * k_hat, axis=(0, 1)))
    grad_q = norm_back(grad_qn * q_gain.astype(jnp.float32), q_hat, q_inv)
    grad_k = norm_back(grad_kn * k_gain.astype(jnp.float32), k_hat, k_inv)
    return (out_bf, grad_q, grad_k, grad_v, q_gain_grad, k_gain_grad)

def reference(activations, cotangent, ln_gain, w_in, w_out, q_gain, k_gain):
    head_width = HEADS_DEV * HEAD_DIM
    groups = N_MP * HEADS_DEV
    w_groups = w_in.reshape(D, N_MP, C_DEV).astype(jnp.float32)

    def as_heads(block):
        return block.reshape(IMG_DEV, PATCHES, groups, HEAD_DIM)

    def as_rows(block):
        return block.reshape(TOK_DEV, N_MP, head_width)

    def replica(totals, inputs):
        acc_in, acc_out, acc_ln, acc_q, acc_k = totals
        x_rows, dy_rows = inputs
        x_hat, x_inv = normalize(x_rows.astype(jnp.float32))
        x_normed = (x_hat * ln_gain.astype(jnp.float32)).astype(jnp.bfloat16)
        projected = jnp.dot(x_normed, w_in, preferred_element_type=jnp.float32).reshape(TOK_DEV, N_MP, C_DEV)
        grad_cat = jnp.dot(dy_rows, w_out.T, preferred_element_type=jnp.float32).reshape(TOK_DEV, N_MP, C_OUT_DEV)
        grad_out_bf = as_heads(grad_cat[:, :, :head_width].astype(jnp.bfloat16))
        out_bf, grad_q, grad_k, grad_v, q_gain_grad, k_gain_grad = attend(as_heads(projected[:, :, :head_width]), as_heads(projected[:, :, head_width:2 * head_width]), as_heads(projected[:, :, 2 * head_width:3 * head_width]), grad_out_bf, q_gain, k_gain)
        activation, gelu_slope = gelu_pair(projected[:, :, 3 * head_width:])
        act_bf = activation.astype(jnp.bfloat16)
        grad_pre = grad_cat[:, :, head_width:] * gelu_slope
        joined = jnp.concatenate([as_rows(out_bf), act_bf], axis=2).reshape(TOK_DEV, C_OUT)
        acc_out = acc_out + jnp.dot(joined.T, dy_rows, preferred_element_type=jnp.float32)
        grad_proj = jnp.concatenate([as_rows(grad_q), as_rows(grad_k), as_rows(grad_v), grad_pre], axis=2).astype(jnp.bfloat16)
        in_part = jnp.dot(x_normed.T, grad_proj.reshape(TOK_DEV, C_IN), preferred_element_type=jnp.float32).astype(jnp.bfloat16)
        acc_in = acc_in + lax.optimization_barrier(in_part).astype(jnp.float32)
        pieces = jnp.einsum('tsc,dsc->tsd', grad_proj.astype(jnp.float32), w_groups).astype(jnp.bfloat16)
        grad_xn = lax.optimization_barrier(jnp.sum(lax.optimization_barrier(pieces).astype(jnp.float32), axis=1))
        acc_ln = acc_ln + lax.optimization_barrier(jnp.sum(grad_xn * x_hat, axis=0))
        scaled = grad_xn * ln_gain.astype(jnp.float32)
        dx_rows = (dy_rows.astype(jnp.float32) + norm_back(scaled, x_hat, x_inv)).astype(jnp.bfloat16)
        return ((acc_in, acc_out, acc_ln, acc_q + q_gain_grad, acc_k + k_gain_grad), dx_rows)
    start_totals = (jnp.zeros((D, C_IN), jnp.float32), jnp.zeros((C_OUT, D), jnp.float32), jnp.zeros((D,), jnp.float32), jnp.zeros((HEADS, HEAD_DIM), jnp.float32), jnp.zeros((HEADS, HEAD_DIM), jnp.float32))
    totals, dx_all = lax.scan(replica, start_totals, (activations.reshape(N_DP, TOK_DEV, D), cotangent.reshape(N_DP, TOK_DEV, D)))
    acc_in, acc_out, acc_ln, acc_q, acc_k = totals
    factor = 1.0 / N_DP
    return (dx_all.reshape(TOKENS, D), (acc_in * factor).astype(jnp.bfloat16), (acc_out * factor).astype(jnp.bfloat16), acc_ln * factor, acc_q * factor, acc_k * factor)
```

```python
import jax
import jax.numpy as jnp
from jax import lax
from jax.experimental import pallas as pl
from jax.experimental.pallas import tpu as pltpu
from jax.sharding import PartitionSpec as P

F32 = jnp.float32
BF16 = jnp.bfloat16
EPS = 1e-6
RING = 8
WIDTH = 3072
FACTOR = 1.0 / 32.0


def dot(a, b):
    return jnp.dot(a, b, preferred_element_type=F32)


def dot_t(a, b):
    return lax.dot_general(a, b, (((1,), (1,)), ((), ())), preferred_element_type=F32)


def roll64(v):
    return pltpu.roll(v, 64, 1)


def low_lanes(rows):
    return lax.broadcasted_iota(jnp.int32, (rows, 128), 1) < 64


def normalize(v):
    mean = jnp.mean(v, axis=-1, keepdims=True)
    cen = v - mean
    inv = lax.rsqrt(jnp.mean(cen * cen, axis=-1, keepdims=True) + EPS)
    return cen * inv, inv


def norm_back(u, hat, inv):
    m0 = jnp.mean(u, axis=-1, keepdims=True)
    m1 = jnp.mean(u * hat, axis=-1, keepdims=True)
    return inv * (u - m0 - hat * m1)


def chain_len(d, b):
    return 4 if d == b else 3


def slot(d, b, s):
    return d * 8 + b * 4 + s


def kernel(
    act_h, cot_h, gain_h, win_h, wout_h, qg_h, kg_h,
    gx_ref, gwi_ref, gwo_ref, gs_ref,
    act_v, cot_v, gain_v, wout, qg_v, kg_v,
    wf, xg, xs, xn, xt, xts, dy2, ot, jt, gp2,
    in_snd, in_rcv, out_snd, out_rcv, dxt, dxr, ps, ga, gb,
    ld, w_s, w_r, wc_s, wc_r, x_s, x_r, sb_s, sb_r,
    i_s, i_r, o_s, o_r, a_s, a_r, ac_s, ac_r, d_s, d_r, p_s, p_r, g_s, g_r,
):
    dp = lax.axis_index("dp")
    mp = lax.axis_index("mp")
    y, h, c = dp // 4, (dp // 2) % 2, dp % 2
    l, z = mp // RING, mp % RING

    def wrap(i):
        return lax.rem(i + 2 * RING, RING)

    def dpi(yy, hh, cc):
        return (wrap(yy) * 2 + hh) * 2 + cc

    def mpi(ll, zz):
        return ll * RING + wrap(zz)

    def on_dp(yy, hh, cc):
        return {"dp": dpi(yy, hh, cc), "mp": mp}

    def on_mp(ll, zz):
        return {"dp": dp, "mp": mpi(ll, zz)}

    sibling = on_dp(y, h, 1 - c)
    even = z % 2

    loads = []
    for i, (src, dst) in enumerate(
        ((act_h, act_v), (cot_h, cot_v), (gain_h, gain_v), (win_h, wf.at[dp]), (qg_h, qg_v), (kg_h, kg_v), (wout_h, wout))
    ):
        cp = pltpu.make_async_copy(src, dst, ld.at[i])
        cp.start()
        loads.append(cp)

    barrier = pltpu.get_barrier_semaphore()
    peers = [on_dp(y + k, h, c) for k in range(1, RING)]
    peers += [sibling, on_dp(y, 1 - h, c), on_dp(y, 1 - h, 1 - c), on_dp(y + 1, 1 - h, c), on_dp(y - 1, 1 - h, c)]
    peers += [on_mp(l, z + k) for k in range(1, RING)] + [on_mp(1 - l, z + k) for k in range(RING)]
    for p in peers:
        pl.semaphore_signal(barrier, inc=1, device_id=p, device_id_type=pl.DeviceIdType.MESH)

    def natural_to_packed(n0, n1, rows):
        lo = low_lanes(rows)
        ev = jnp.full((rows, 128), even, jnp.int32) == 0
        r0, r1 = roll64(n0), roll64(n1)
        return jnp.where(ev, n0, jnp.where(lo, r0, r1)), jnp.where(ev, n1, r0)

    lo64 = low_lanes(64)
    ev64 = jnp.full((64, 128), even, jnp.int32) == 0
    first64 = lo64 == ev64
    lo128 = low_lanes(128)
    valid128 = lo128 == (jnp.full((128, 128), even, jnp.int32) == 0)

    for i in range(3):
        loads[i].wait()
    for src, base in ((act_v, 0), (cot_v, 192)):
        n0 = src[:, 0:128].astype(F32)
        t = src[:, 128:192].astype(F32)
        n1 = jnp.concatenate([t, t], axis=1)
        full, half = natural_to_packed(n0, n1, 128)
        xg[mp, base : base + 128, :] = full.astype(BF16)
        xg[mp, base + 128 : base + 192, :] = jnp.where(first64, half[0:64], roll64(half[64:128])).astype(BF16)
    t = jnp.broadcast_to(gain_v[:, 128:192], (8, 64))
    gain_full, gain_half = natural_to_packed(
        jnp.broadcast_to(gain_v[:, 0:128], (8, 128)), jnp.concatenate([t, t], axis=1), 8
    )
    xg[mp, 384:400, :] = jnp.concatenate([gain_full, gain_half], axis=0).astype(BF16)
    loads[3].wait()
    pl.semaphore_wait(barrier, len(peers))

    pending = []

    def remote(src, dst, snd, rcv, to):
        return pltpu.make_async_remote_copy(
            src_ref=src, dst_ref=dst, send_sem=snd, recv_sem=rcv, device_id=to, device_id_type=pl.DeviceIdType.MESH
        )

    def send(src, dst, snd, rcv, to):
        cp = remote(src, dst, snd, rcv, to)
        cp.start()
        pending.append(cp)

    class Gather:
        def __init__(self, blk, snd, rcv, up, down, up_x, down_x, pair, forward=None):
            self.blk, self.snd, self.rcv = blk, snd, rcv
            self.to = ((up, up_x), (down, down_x))
            self.near = (up, down)
            self.pair, self.forward = pair, forward
            self.n_fwd = 0

        def _fwd(self, off, b):
            if self.forward is not None:
                s, r = self.forward
                ref = self.blk(off, b)
                send(ref, ref, s.at[self.n_fwd], r.at[self.n_fwd], sibling)
                self.n_fwd += 1

        def start(self):
            own = self.blk(0, 0)
            for b in range(2):
                for d in range(2):
                    i = slot(d, b, 0)
                    send(own, own, self.snd.at[i], self.rcv.at[i], self.to[d][b])
                if b == 0:
                    send(own, own, self.snd.at[16], self.rcv.at[16], self.pair)
            self._fwd(0, 0)

        def arrive(self, off, b, i, to):
            ref = self.blk(off, b)
            remote(ref, ref, self.snd.at[i], self.rcv.at[i], to).wait_recv()

        def step(self, st):
            for b in range(2):
                for d in range(2):
                    if st == 4 and d != b:
                        continue
                    off = -st if d == 0 else st
                    self.arrive(off, b, slot(d, b, st - 1), self.near[d])
                    if st < 3 or (st == 3 and d == b):
                        i = slot(d, b, st)
                        ref = self.blk(off, b)
                        send(ref, ref, self.snd.at[i], self.rcv.at[i], self.near[d])
                    self._fwd(off, b)
            if st == 1:
                self.arrive(0, 1, 16, self.pair)
                self._fwd(0, 1)

    def half_h(b):
        return h if b == 0 else 1 - h

    def half_l(b):
        return l if b == 0 else 1 - l

    y_near = (on_dp(y + 1, h, c), on_dp(y - 1, h, c), on_dp(y + 1, 1 - h, c), on_dp(y - 1, 1 - h, c), on_dp(y, 1 - h, c))
    z_near = (on_mp(l, z + 1), on_mp(l, z - 1), on_mp(1 - l, z + 1), on_mp(1 - l, z - 1), on_mp(1 - l, z))
    gx_ring = Gather(lambda off, b: xg.at[mpi(half_l(b), z + off)], x_s, x_r, *z_near)
    gw_ring = Gather(lambda off, b: wf.at[dpi(y + off, half_h(b), c)], w_s, w_r, *y_near, forward=(wc_s, wc_r))

    gx_ring.start()
    gw_ring.start()

    for i in range(4, 7):
        loads[i].wait()

    def unpack(j, base):
        ea, eb = 2 * j, 2 * j + 1
        a = xg[ea, base + 128 : base + 192, :].astype(F32)
        b = xg[eb, base + 128 : base + 192, :].astype(F32)
        mid = jnp.concatenate([jnp.where(lo64, a, b), roll64(jnp.where(lo64, b, a))], axis=0)
        return (xg[ea, base : base + 128, :], mid, xg[eb, base : base + 128, :])

    def process(q, carry):
        gcat, sums = carry
        for b in range(2):
            j = half_l(b) * 4 + lax.rem(z // 2 + q + 4, 4)
            x0, xm, x2 = unpack(j, 0)
            x0, x2 = x0.astype(F32), x2.astype(F32)
            xs[j, :, 0:128] = x0
            xs[j, :, 128:256] = xm
            xs[j, :, 256:384] = x2
            sums = sums + (x0 + xm + x2)
            d0, dm, d2 = unpack(j, 192)
            dy = jnp.concatenate([d0, dm.astype(BF16), d2], axis=1)
            dy2[j, 0:128, :] = dy
            gcat = gcat + dot_t(dy, wout[:, pl.ds(pl.multiple_of(j * 384, 128), 384)])
        return gcat, sums

    carry = (jnp.zeros((128, 256), F32), jnp.zeros((128, 128), F32))
    for st in range(1, 5):
        gx_ring.step(st)
        gw_ring.step(st)
        if st == 1:
            carry = process(0, carry)
        if st == 3:
            carry = process(1, carry)
            carry = process(-1, carry)
        if st == 4:
            carry = process(2, carry)
    grad_cat, sums = carry
    send(dy2.at[:, 0:128], dy2.at[:, 128:256], sb_s.at[0], sb_r.at[0], sibling)

    x_mean = jnp.sum(sums, axis=-1, keepdims=True) * (1.0 / WIDTH)

    def var_body(j, acc):
        v = xs[j] - x_mean
        v = v * v
        return acc + (v[:, 0:128] + v[:, 128:256] + v[:, 256:384])

    var = lax.fori_loop(0, 8, var_body, jnp.zeros((128, 128), F32))
    x_inv = lax.rsqrt(jnp.sum(var, axis=-1, keepdims=True) * (1.0 / WIDTH) + EPS)

    for i in range(16):
        ref = wf.at[0]
        remote(ref, ref, wc_s.at[i], wc_r.at[i], sibling).wait_recv()

    def proj_body(j, acc):
        ga_ = xg[2 * j, 384:400, :].astype(F32)
        gb_ = xg[2 * j + 1, 384:400, :].astype(F32)
        gm = jnp.where(low_lanes(1), ga_[8:9], gb_[8:9])
        gain = jnp.concatenate([ga_[0:1], gm, gb_[0:1]], axis=1)
        v = (xs[j] - x_mean) * x_inv * gain
        vb = v.astype(BF16)
        xn[j] = vb
        w = wf[pl.ds(4 * j, 4)].reshape(384, 512)
        return acc + dot(vb, w)

    proj = lax.fori_loop(0, 8, proj_body, jnp.zeros((128, 512), F32))

    pre = proj[:, 384:512]
    cdf = 0.5 * (1.0 + lax.erf(pre * 0.7071067811865476))
    pdf = jnp.exp(-0.5 * pre * pre) * 0.3989422804014327
    act = pre * cdf
    grad_pre = grad_cat[:, 128:256] * (cdf + pre * pdf)

    scaling = 128.0 ** -0.5
    qg, kg = qg_v[...].astype(F32), kg_v[...].astype(F32)
    q_hat, q_inv = normalize(proj[:, 0:128])
    k_hat, k_inv = normalize(proj[:, 128:256])
    qn, kn = (q_hat * qg).astype(BF16), (k_hat * kg).astype(BF16)
    v_bf = proj[:, 256:384].astype(BF16)
    go = grad_cat[:, 0:128].astype(BF16)
    sc = dot_t(qn, kn) * scaling
    e = jnp.exp(sc - jnp.max(sc, axis=-1, keepdims=True))
    prob = e / jnp.sum(e, axis=-1, keepdims=True)
    out = dot(prob.astype(BF16), v_bf)

    is0 = jnp.full((128, 128), c, jnp.int32) == 0
    jt[0] = jnp.where(is0, out, act).T.astype(BF16)
    jt[1] = jnp.where(is0, act, out).T.astype(BF16)
    send(jt.at[1], jt.at[2], sb_s.at[1], sb_r.at[1], sibling)

    gprob = dot_t(go, v_bf)
    grad_v = dot(prob.T.astype(BF16), go)
    gsc = prob * (gprob - jnp.sum(prob * gprob, axis=-1, keepdims=True)) * scaling
    gqn = dot(gsc.astype(BF16), kn)
    gkn = dot(gsc.T.astype(BF16), qn)
    gqg = jnp.sum(gqn * q_hat, axis=0, keepdims=True)
    gkg = jnp.sum(gkn * k_hat, axis=0, keepdims=True)
    grad_q = norm_back(gqn * qg, q_hat, q_inv)
    grad_k = norm_back(gkn * kg, k_hat, k_inv)
    gp = jnp.concatenate([grad_q, grad_k, grad_v, grad_pre], axis=1).astype(BF16)
    gp2[0] = gp
    send(gp2.at[0], gp2.at[1], sb_s.at[2], sb_r.at[2], sibling)

    def xt_body(j, _):
        t = xn[j].astype(F32)
        t = jnp.concatenate([t[:, k * 128 : (k + 1) * 128].T for k in range(3)], axis=0).astype(BF16)
        xt[pl.ds(2 * j, 2)] = t.reshape(2, 2, 96, 128)
        return 0

    lax.fori_loop(0, 8, xt_body, 0)
    send(xt.at[:, 1 - c], xts, sb_s.at[3], sb_r.at[3], sibling)

    def dx_body(j, _):
        w = wf[pl.ds(4 * j, 4)].reshape(384, 512)
        t = dot_t(gp2[0], w)
        mid = t[:, 128:256]
        top, bottom = mid[0:64], roll64(mid[64:128])
        dxt[2 * j, 0:128, :] = t[:, 0:128].astype(BF16)
        dxt[2 * j, 128:192, :] = jnp.where(lo64, top, bottom).astype(BF16)
        dxt[2 * j + 1, 0:128, :] = t[:, 256:384].astype(BF16)
        dxt[2 * j + 1, 128:192, :] = jnp.where(lo64, bottom, top).astype(BF16)
        return 0

    lax.fori_loop(0, 8, dx_body, 0)
    mp_peers = [(b, k) for k in (4, 3, 5, 2, 6, 1, 7, 0) for b in range(2) if (b, k) != (0, 0)]
    for b, k in mp_peers:
        i = b * 8 + k
        send(dxt.at[mpi(half_l(b), z + k)], dxr.at[i], d_s.at[i], d_r.at[i], on_mp(half_l(b), z + k))

    remote(jt.at[1], jt.at[2], sb_s.at[1], sb_r.at[1], sibling).wait_recv()
    remote(dy2.at[:, 0:128], dy2.at[:, 128:256], sb_s.at[0], sb_r.at[0], sibling).wait_recv()
    jt_cat = jnp.concatenate([jt[0], jt[2]], axis=1)

    def ot_body(j, _):
        t = dot(jt_cat, dy2[j])
        ot[pl.ds(2 * j, 2)] = t.reshape(2, 64, 384)
        return 0

    lax.fori_loop(0, 8, ot_body, 0)

    class Reduce:
        def __init__(self, term, snd, rcv, s, r, near, pair):
            self.term, self.snd, self.rcv, self.s, self.r = term, snd, rcv, s, r
            self.near, self.pair = near, pair

        def _send(self, i, value, to):
            self.snd[i] = value.astype(BF16)
            send(self.snd.at[i], self.rcv.at[i], self.s.at[i], self.r.at[i], to)

        def _arrived(self, i, to):
            remote(self.snd.at[i], self.rcv.at[i], self.s.at[i], self.r.at[i], to).wait_recv()
            return self.rcv[i].astype(F32)

        def step(self, st):
            for b in range(2):
                for d in range(2):
                    n = chain_len(d, b)
                    if st >= n:
                        continue
                    off = (n - st) if d == 0 else st - n
                    value = self.term(off, b)
                    if st > 0:
                        value = value + self._arrived(slot(d, b, st - 1), self.near[d])
                    self._send(slot(d, b, st), value, self.near[d])

        def total(self, b):
            value = self.term(0, b)
            for d in range(2):
                value = value + self._arrived(slot(d, b, chain_len(d, b) - 1), self.near[d])
            return value

        def finish(self):
            self._send(7, self.total(1), self.pair)
            return self.total(0)

        def partner(self):
            return self._arrived(7, self.pair)

    def term_out(off, b):
        return ot[wrap(y + off) * 2 + half_h(b)]

    def term_in(off, b):
        i = wrap(y + off) * 2 + half_h(b)
        return dot(jnp.concatenate([xt[i, c], xts[i]], axis=1), gp2[...].reshape(256, 512))

    ring_out = Reduce(term_out, out_snd, out_rcv, o_s, o_r, y_near[0:2], y_near[4])
    ring_in = Reduce(term_in, in_snd, in_rcv, i_s, i_r, y_near[0:2], y_near[4])

    ring_out.step(0)
    remote(gp2.at[0], gp2.at[1], sb_s.at[2], sb_r.at[2], sibling).wait_recv()
    remote(xt.at[:, 1 - c], xts, sb_s.at[3], sb_r.at[3], sibling).wait_recv()
    ring_in.step(0)
    for st in range(1, 4):
        ring_out.step(st)
        ring_in.step(st)
    out_sum = ring_out.finish()

    dxn = dxt[mp].astype(F32)
    for b, k in mp_peers:
        i = b * 8 + k
        remote(dxt.at[0], dxr.at[i], d_s.at[i], d_r.at[i], on_mp(half_l(b), z + k)).wait_recv()
        dxn = dxn + dxr[i].astype(F32)

    def tiles(packed):
        half = packed[128:192]
        return packed[0:128], jnp.where(valid128, jnp.concatenate([half, roll64(half)], axis=0), 0.0)

    own = xg[mp].astype(F32)
    x_full, x_half = tiles(own[0:192])
    dx_full, dx_half = tiles(dxn)
    hat_full = (x_full - x_mean) * x_inv
    hat_half = jnp.where(valid128, (x_half - x_mean) * x_inv, 0.0)
    ln_full = jnp.sum(dx_full * hat_full, axis=0, keepdims=True)
    ln_half = jnp.sum(dx_half * hat_half, axis=0, keepdims=True)
    s_full, s_half = dx_full * own[384:385], dx_half * jnp.where(low_lanes(1) == (jnp.full((1, 128), even, jnp.int32) == 0), own[392:393], 0.0)
    sum0 = jnp.sum(s_full + s_half, axis=-1, keepdims=True)
    sum1 = jnp.sum(s_full * hat_full + s_half * hat_half, axis=-1, keepdims=True)
    lane128 = lax.broadcasted_iota(jnp.int32, (128, 128), 1)
    cols = jnp.where(lane128 == 0, sum0, jnp.where(lane128 == 1, sum1, 0.0))
    ps[0] = cols.T[0:8]
    for b, k in mp_peers:
        i = b * 8 + k
        send(ps.at[0], ps.at[i], p_s.at[i], p_r.at[i], on_mp(half_l(b), z + k))

    ga[0] = jnp.concatenate([gqg, gkg, ln_full, ln_half, jnp.zeros((4, 128), F32)], axis=0)
    quad = (on_dp(y, h, 1 - c), on_dp(y, 1 - h, c), on_dp(y, 1 - h, 1 - c))
    for i, p in enumerate(quad):
        send(ga.at[0], ga.at[i + 1], g_s.at[i], g_r.at[i], p)

    def blk_out(off, b):
        return gwo_ref.at[dpi(y + off, half_h(b), c)]

    gwo_ref[dp] = ((out_sum + ring_out.partner()) * FACTOR).astype(BF16)
    ga_ring = Gather(blk_out, a_s, a_r, *y_near, forward=(ac_s, ac_r))
    ga_ring.start()

    in_sum = ring_in.finish()

    for i, p in enumerate(quad):
        remote(ga.at[0], ga.at[i + 1], g_s.at[i], g_r.at[i], p).wait_recv()
    gb[0] = (ga[0] + ga[1]) + (ga[2] + ga[3])
    for k in range(1, RING):
        send(gb.at[0], gb.at[k], g_s.at[2 + k], g_r.at[2 + k], on_dp(y + k, h, c))

    ga_ring.step(1)

    acc = ps[0]
    for b, k in mp_peers:
        i = b * 8 + k
        remote(ps.at[0], ps.at[i], p_s.at[i], p_r.at[i], on_mp(half_l(b), z + k)).wait_recv()
        acc = acc + ps[i]
    back = (jnp.concatenate([acc, jnp.zeros((120, 128), F32)], axis=0) * (1.0 / WIDTH)).T
    mean0, mean1 = back[:, 0:1], back[:, 1:2]
    c_full, c_half = tiles(own[192:384])
    r_full = c_full + x_inv * (s_full - mean0 - hat_full * mean1)
    r_half = c_half + x_inv * (s_half - mean0 - hat_half * mean1)

    def packed_to_natural(full, half, rows):
        ev = jnp.full((rows, 128), even, jnp.int32) == 0
        rf = roll64(full)
        return jnp.where(ev, full, jnp.where(low_lanes(rows), roll64(half), rf)), jnp.where(ev, half, rf)

    o0, o1 = packed_to_natural(r_full, r_half, 128)
    gx_ref[:, 0:128] = o0.astype(BF16)
    gx_ref[:, 128:192] = o1[:, 0:64].astype(BF16)

    ga_ring.step(2)
    gwi_ref[...] = ((in_sum + ring_in.partner()) * FACTOR).astype(BF16)
    ga_ring.step(3)
    total = gb[0]
    for k in range(1, RING):
        remote(gb.at[0], gb.at[k], g_s.at[2 + k], g_r.at[2 + k], on_dp(y + k, h, c)).wait_recv()
        total = total + gb[k]
    total = total * FACTOR
    g0, g1 = packed_to_natural(
        jnp.broadcast_to(total[2:3], (8, 128)), jnp.broadcast_to(total[3:4], (8, 128)), 8
    )
    gs_ref[...] = jnp.concatenate([total[0:2], g0[0:1], g1[0:1], jnp.zeros((4, 128), F32)], axis=0)
    ga_ring.step(4)
    for i in range(16):
        ref = gwo_ref.at[0]
        remote(ref, ref, ac_s.at[i], ac_r.at[i], sibling).wait_recv()
    for cp in pending:
        cp.wait_send()


def per_device(activations, cotangent, ln_gain, w_in, w_out, q_gain, k_gain):
    any_space = pl.BlockSpec(memory_space=pl.ANY)
    vmem = pl.BlockSpec(memory_space=pltpu.VMEM)
    dma = pltpu.SemaphoreType.DMA

    def buf(*shape, dtype=BF16):
        return pltpu.VMEM(shape, dtype)

    scratch = [
        buf(128, 192), buf(128, 192), buf(1, 192, dtype=F32), buf(256, 3072), buf(1, 128), buf(1, 128),
        buf(32, 96, 512),
        buf(16, 400, 128),
        buf(8, 128, 384, dtype=F32),
        buf(8, 128, 384),
        buf(16, 2, 96, 128), buf(16, 96, 128),
        buf(8, 256, 384),
        buf(16, 64, 384, dtype=F32),
        buf(3, 128, 128),
        buf(2, 128, 512),
        buf(16, 96, 512), buf(16, 96, 512), buf(16, 64, 384), buf(16, 64, 384),
        buf(16, 192, 128), buf(16, 192, 128),
        buf(16, 8, 128, dtype=F32), buf(4, 8, 128, dtype=F32), buf(8, 8, 128, dtype=F32),
        dma((7,)), dma((17,)), dma((17,)), dma((16,)), dma((16,)), dma((17,)), dma((17,)), dma((4,)), dma((4,)),
        dma((16,)), dma((16,)), dma((16,)), dma((16,)), dma((17,)), dma((17,)), dma((16,)), dma((16,)),
        dma((16,)), dma((16,)), dma((16,)), dma((16,)), dma((10,)), dma((10,)),
    ]
    grad_x, grad_w_in, grad_w_out, sums = pl.pallas_call(
        kernel,
        out_shape=(
            jax.ShapeDtypeStruct((128, 192), BF16),
            jax.ShapeDtypeStruct((96, 512), BF16),
            jax.ShapeDtypeStruct((32, 64, 384), BF16),
            jax.ShapeDtypeStruct((8, 128), F32),
        ),
        in_specs=[any_space] * 7,
        out_specs=(vmem,) * 4,
        scratch_shapes=scratch,
        compiler_params=pltpu.CompilerParams(collective_id=0, has_side_effects=True, vmem_limit_bytes=48 << 20),
    )(activations, cotangent, ln_gain.astype(F32).reshape(1, 192), w_in, w_out, q_gain, k_gain)
    grad_w_out = grad_w_out.reshape(8, 2, 2, 64, 384).transpose(2, 1, 3, 0, 4).reshape(256, 3072)
    grad_ln = jnp.concatenate([sums[2], sums[3, 0:64]])
    return grad_x, grad_w_in, grad_w_out, grad_ln, sums[0:1], sums[1:2]


def solution(mesh):
    in_specs = (P("dp", "mp"), P("dp", "mp"), P("mp"), P("dp", "mp"), P("mp", None), P("mp", None), P("mp", None))
    out_specs = (P("dp", "mp"), P("dp", "mp"), P("mp", None), P("mp"), P("mp", None), P("mp", None))
    return jax.shard_map(per_device, mesh=mesh, in_specs=in_specs, out_specs=out_specs, check_vma=False)
```

```python
import jax
import jax.numpy as jnp
from jax import lax
from jax.experimental import pallas as pl
from jax.experimental.pallas import tpu as pltpu
from jax.sharding import PartitionSpec as P

F32 = jnp.float32
BF16 = jnp.bfloat16
EPS = 1e-6
RING = 8
WIDTH = 3072
FACTOR = 1.0 / 32.0


def dot(a, b):
    return jnp.dot(a, b, preferred_element_type=F32)


def dot_t(a, b):
    return lax.dot_general(a, b, (((1,), (1,)), ((), ())), preferred_element_type=F32)


def normalize(v):
    mean = jnp.mean(v, axis=-1, keepdims=True)
    cen = v - mean
    inv = lax.rsqrt(jnp.mean(cen * cen, axis=-1, keepdims=True) + EPS)
    return cen * inv, inv


def norm_back(u, hat, inv):
    m0 = jnp.mean(u, axis=-1, keepdims=True)
    m1 = jnp.mean(u * hat, axis=-1, keepdims=True)
    return inv * (u - m0 - hat * m1)


def rows8(v):
    return jnp.sum(v.reshape(v.shape[0] // 8, 8, 128), axis=0)


def row_of(column):
    return jnp.broadcast_to(column, (128, 128)).T[0:1]


def column_of(row):
    return jnp.broadcast_to(row, (128, 128)).T


def chain_len(d, b):
    return 4 if d == b else 3


def slot(d, b, s):
    return d * 8 + b * 4 + s


def kernel(
    act_h, cot_h, gain_h, win_h, wout_h, qg_h, kg_h,
    gx_ref, gwi_ref, gwo_ref, gs_ref,
    gain_v, wout, qg_v, kg_v,
    wf, xg, xt, xts, dys, ot, jt, gp2,
    in_snd, in_rcv, out_snd, out_rcv, dxt, dxr, ps, ga, gb,
    ld, w_s, w_r, wc_s, wc_r, x_s, x_r, sb_s, sb_r,
    i_s, i_r, o_s, o_r, a_s, a_r, ac_s, ac_r, d_s, d_r, p_s, p_r, g_s, g_r,
):
    dp = lax.axis_index("dp")
    mp = lax.axis_index("mp")
    y, h, c = dp // 4, (dp // 2) % 2, dp % 2
    l, z = mp // RING, mp % RING

    def wrap(i):
        return lax.rem(i + 2 * RING, RING)

    def dpi(yy, hh, cc):
        return (wrap(yy) * 2 + hh) * 2 + cc

    def mpi(ll, zz):
        return ll * RING + wrap(zz)

    def on_dp(yy, hh, cc):
        return {"dp": dpi(yy, hh, cc), "mp": mp}

    def on_mp(ll, zz):
        return {"dp": dp, "mp": mpi(ll, zz)}

    sibling = on_dp(y, h, 1 - c)

    loads = []
    for i, (src, dst) in enumerate(
        ((gain_h, gain_v), (act_h, xg.at[mp, 0:192]), (cot_h, xg.at[mp, 192:384]), (win_h, wf.at[dp]), (qg_h, qg_v), (kg_h, kg_v), (wout_h, wout))
    ):
        cp = pltpu.make_async_copy(src, dst, ld.at[i])
        cp.start()
        loads.append(cp)

    barrier = pltpu.get_barrier_semaphore()
    peers = [on_dp(y + k, h, c) for k in range(1, RING)]
    peers += [sibling, on_dp(y, 1 - h, c), on_dp(y, 1 - h, 1 - c), on_dp(y + 1, 1 - h, c), on_dp(y - 1, 1 - h, c)]
    peers += [on_mp(l, z + k) for k in range(1, RING)] + [on_mp(1 - l, z + k) for k in range(RING)]
    for p in peers:
        pl.semaphore_signal(barrier, inc=1, device_id=p, device_id_type=pl.DeviceIdType.MESH)

    loads[0].wait()
    gain = gain_v[...].astype(F32).reshape(1, 192)
    gain0 = gain[:, 0:128]
    gain1 = jnp.concatenate([gain[:, 128:192], gain[:, 128:192]], axis=1)
    xg[mp, 384:400, :] = jnp.concatenate(
        [jnp.broadcast_to(gain0, (8, 128)), jnp.broadcast_to(gain1, (8, 128))], axis=0
    ).astype(BF16)
    for i in range(1, 4):
        loads[i].wait()
    pl.semaphore_wait(barrier, len(peers))

    def remote(src, dst, snd, rcv, to):
        return pltpu.make_async_remote_copy(
            src_ref=src, dst_ref=dst, send_sem=snd, recv_sem=rcv, device_id=to, device_id_type=pl.DeviceIdType.MESH
        )

    def send(src, dst, snd, rcv, to):
        remote(src, dst, snd, rcv, to).start()

    def wait_bytes(ref, sem):
        pltpu.make_async_copy(ref, ref, sem).wait()

    class Gather:
        def __init__(self, blk, snd, rcv, near, forward=None):
            self.blk, self.snd, self.rcv = blk, snd, rcv
            self.near, self.pair, self.forward = near[0:2], near[2], forward

        def _fwd(self, off, b):
            if self.forward is not None:
                s, r = self.forward
                ref = self.blk(off, b)
                send(ref, ref, s, r, sibling)

        def _send(self, off, b, i, to):
            ref = self.blk(off, b)
            send(ref, ref, self.snd, self.rcv.at[i], to)

        def start(self):
            self._send(0, 0, 7, self.pair)
            for d in range(2):
                self._send(0, 0, slot(d, 0, 0), self.near[d])
            self._fwd(0, 0)

        def start_partner(self):
            self.arrive(0, 1, 7, self.pair)
            for d in range(2):
                self._send(0, 1, slot(d, 1, 0), self.near[d])
            self._fwd(0, 1)

        def arrive(self, off, b, i, to):
            ref = self.blk(off, b)
            remote(ref, ref, self.snd, self.rcv.at[i], to).wait_recv()

        def step(self, st, b):
            for d in range(2):
                n = chain_len(d, b)
                if st > n:
                    continue
                off = -st if d == 0 else st
                self.arrive(off, b, slot(d, b, st - 1), self.near[d])
                if st < n:
                    self._send(off, b, slot(d, b, st), self.near[d])
                self._fwd(off, b)

    def start_rings(rings):
        for r in rings:
            r.start()
        for r in rings:
            r.start_partner()

    def step_rings(rings, st):
        for b in range(2):
            for r in rings:
                r.step(st, b)

    def half_h(b):
        return h if b == 0 else 1 - h

    def half_l(b):
        return l if b == 0 else 1 - l

    y_near = (on_dp(y + 1, h, c), on_dp(y - 1, h, c), on_dp(y, 1 - h, c))
    z_near = (on_mp(l, z + 1), on_mp(l, z - 1), on_mp(1 - l, z))
    gx_ring = Gather(lambda off, b: xg.at[mpi(half_l(b), z + off)], x_s, x_r, z_near)
    gw_ring = Gather(lambda off, b: wf.at[dpi(y + off, half_h(b), c)], w_s, w_r, y_near, forward=(wc_s, wc_r))
    start_rings((gx_ring, gw_ring))

    for i in range(4, 7):
        loads[i].wait()

    def process(q, carry):
        gcat, sums = carry
        for b in range(2):
            j = half_l(b) * 4 + lax.rem(z // 2 + q + 4, 4)
            pair = xg[pl.ds(2 * j, 2)]
            sums = sums + rows8(pair[:, 0:192].reshape(384, 128).astype(F32))
            dy = pair[:, 192:384].reshape(384, 128)
            gcat = gcat + dot(wout[:, pl.ds(pl.multiple_of(j * 384, 128), 384)], dy)
        return gcat, sums

    carry = (jnp.zeros((256, 128), F32), jnp.zeros((8, 128), F32))
    for st in range(1, 5):
        step_rings((gx_ring, gw_ring), st)
        if st == 1:
            carry = process(0, carry)
        if st == 3:
            carry = process(1, carry)
            carry = process(-1, carry)
        if st == 4:
            carry = process(2, carry)
    grad_cat, sums = carry
    send(xg.at[:, 192:384], dys, sb_s.at[0], sb_r.at[0], sibling)

    x_mean = jnp.sum(sums, axis=0, keepdims=True) * (1.0 / WIDTH)

    def var_body(m, acc):
        v = xg[m, 0:192, :].astype(F32) - x_mean
        return acc + rows8(v * v)

    var = lax.fori_loop(0, 16, var_body, jnp.zeros((8, 128), F32))
    x_inv = lax.rsqrt(jnp.sum(var, axis=0, keepdims=True) * (1.0 / WIDTH) + EPS)

    gain_rows = []
    for m in range(16):
        t = xg[m, 384:400, :].astype(F32)
        gain_rows += [t[0:1], t[8:9]]
    gains = jnp.concatenate(gain_rows + [jnp.zeros((96, 128), F32)], axis=0).T

    wait_bytes(wf.at[0:16], wc_r)

    proj = jnp.zeros((128, 512), F32)
    for j in range(8):
        parts = []
        for m in (2 * j, 2 * j + 1):
            v = (xg[m, 0:192, :].astype(F32) - x_mean) * x_inv
            top = v[0:128] * gains[:, 2 * m : 2 * m + 1]
            bottom = v[128:192] * gains[0:64, 2 * m + 1 : 2 * m + 2]
            parts += [top, bottom]
        v = jnp.concatenate(parts, axis=0)
        xt[2 * j : 2 * j + 2] = v.astype(BF16).reshape(2, 2, 96, 128)
        vt = jnp.concatenate([v[k * 128 : (k + 1) * 128].T for k in range(3)], axis=1).astype(BF16)
        proj = proj + dot(vt, wf[4 * j : 4 * j + 4].reshape(384, 512))
    send(xt.at[:, 1 - c], xts, sb_s.at[3], sb_r.at[3], sibling)

    pre = proj[:, 384:512]
    cdf = 0.5 * (1.0 + lax.erf(pre * 0.7071067811865476))
    pdf = jnp.exp(-0.5 * pre * pre) * 0.3989422804014327
    act = pre * cdf
    grad_pre = grad_cat[128:256].T * (cdf + pre * pdf)

    scaling = 128.0 ** -0.5
    qg, kg = qg_v[...].astype(F32), kg_v[...].astype(F32)
    q_hat, q_inv = normalize(proj[:, 0:128])
    k_hat, k_inv = normalize(proj[:, 128:256])
    qn, kn = (q_hat * qg).astype(BF16), (k_hat * kg).astype(BF16)
    v_bf = proj[:, 256:384].astype(BF16)
    go = grad_cat[0:128].T.astype(BF16)
    sc = dot_t(qn, kn) * scaling
    e = jnp.exp(sc - jnp.max(sc, axis=-1, keepdims=True))
    prob = e / jnp.sum(e, axis=-1, keepdims=True)
    out = dot(prob.astype(BF16), v_bf)

    is0 = jnp.full((128, 128), c, jnp.int32) == 0
    jt[0] = jnp.where(is0, out, act).T.astype(BF16)
    jt[1] = jnp.where(is0, act, out).T.astype(BF16)
    send(jt.at[1], jt.at[2], sb_s.at[1], sb_r.at[1], sibling)

    gprob = dot_t(go, v_bf)
    grad_v = dot(prob.T.astype(BF16), go)
    gsc = prob * (gprob - jnp.sum(prob * gprob, axis=-1, keepdims=True)) * scaling
    gqn = dot(gsc.astype(BF16), kn)
    gkn = dot(gsc.T.astype(BF16), qn)
    gqg = jnp.sum(gqn * q_hat, axis=0, keepdims=True)
    gkg = jnp.sum(gkn * k_hat, axis=0, keepdims=True)
    grad_q = norm_back(gqn * qg, q_hat, q_inv)
    grad_k = norm_back(gkn * kg, k_hat, k_inv)
    gp = jnp.concatenate([grad_q, grad_k, grad_v, grad_pre], axis=1).astype(BF16)
    gp2[0] = gp
    send(gp2.at[0], gp2.at[1], sb_s.at[2], sb_r.at[2], sibling)

    def dx_body(j, _):
        w = wf[pl.ds(4 * j, 4)].reshape(384, 512)
        dxt[pl.ds(2 * j, 2)] = dot_t(w, gp2[0]).astype(BF16).reshape(2, 192, 128)
        return 0

    lax.fori_loop(0, 8, dx_body, 0)
    mp_peers = [(b, k) for k in (4, 3, 5, 2, 6, 1, 7, 0) for b in range(2) if (b, k) != (0, 0)]
    for b, k in mp_peers:
        i = b * 8 + k
        send(dxt.at[mpi(half_l(b), z + k)], dxr.at[i], d_s, d_r, on_mp(half_l(b), z + k))

    remote(jt.at[1], jt.at[2], sb_s.at[1], sb_r.at[1], sibling).wait_recv()
    remote(xg.at[:, 192:384], dys, sb_s.at[0], sb_r.at[0], sibling).wait_recv()
    jt_cat = jnp.concatenate([jt[0], jt[2]], axis=1)

    def ot_body(j, _):
        own = xg[pl.ds(2 * j, 2), 192:384, :].reshape(384, 128)
        other = dys[pl.ds(2 * j, 2)].reshape(384, 128)
        t = dot_t(jt_cat, jnp.concatenate([own, other], axis=1))
        ot[pl.ds(2 * j, 2)] = t.reshape(2, 64, 384)
        return 0

    lax.fori_loop(0, 8, ot_body, 0)

    class Reduce:
        def __init__(self, term, snd, rcv, s, r, near):
            self.term, self.snd, self.rcv, self.s, self.r = term, snd, rcv, s, r
            self.near, self.pair = near[0:2], near[2]

        def _send(self, i, value, to):
            self.snd[i] = value.astype(BF16)
            send(self.snd.at[i], self.rcv.at[i], self.s, self.r.at[i], to)

        def arrived(self, i, to):
            remote(self.snd.at[i], self.rcv.at[i], self.s, self.r.at[i], to).wait_recv()
            return self.rcv[i].astype(F32)

        def step(self, st):
            for b in range(2):
                for d in range(2):
                    n = chain_len(d, b)
                    if st >= n:
                        continue
                    off = (n - st) if d == 0 else st - n
                    value = self.term(off, b)
                    if st > 0:
                        value = value + self.arrived(slot(d, b, st - 1), self.near[d])
                    self._send(slot(d, b, st), value, self.near[d])

        def total(self, b):
            value = self.term(0, b)
            for d in range(2):
                value = value + self.arrived(slot(d, b, chain_len(d, b) - 1), self.near[d])
            return value

        def finish(self):
            self._send(7, self.total(1), self.pair)
            return self.total(0)

        def partner(self):
            return self.arrived(7, self.pair)

    def term_out(off, b):
        return ot[wrap(y + off) * 2 + half_h(b)]

    def term_in(off, b):
        i = wrap(y + off) * 2 + half_h(b)
        return dot(jnp.concatenate([xt[i, c], xts[i]], axis=1), gp2[...].reshape(256, 512))

    ring_out = Reduce(term_out, out_snd, out_rcv, o_s, o_r, y_near)
    ring_in = Reduce(term_in, in_snd, in_rcv, i_s, i_r, y_near)

    ring_out.step(0)
    remote(gp2.at[0], gp2.at[1], sb_s.at[2], sb_r.at[2], sibling).wait_recv()
    remote(xt.at[:, 1 - c], xts, sb_s.at[3], sb_r.at[3], sibling).wait_recv()
    ring_in.step(0)
    for st in range(1, 4):
        ring_out.step(st)
        ring_in.step(st)
    out_sum = ring_out.finish()

    dxn = dxt[mp].astype(F32)
    wait_bytes(dxr.at[1:16], d_r)
    for i in range(1, 16):
        dxn = dxn + dxr[i].astype(F32)

    own_gain = jnp.concatenate([column_of(gain0), column_of(gain1)[0:64]], axis=0)
    hat = (xg[mp, 0:192, :].astype(F32) - x_mean) * x_inv
    ln_column = jnp.sum(dxn * hat, axis=1, keepdims=True)
    scaled = dxn * own_gain
    sum0 = jnp.sum(scaled, axis=0, keepdims=True)
    sum1 = jnp.sum(scaled * hat, axis=0, keepdims=True)
    ps[0] = jnp.concatenate([sum0, sum1, jnp.zeros((6, 128), F32)], axis=0)
    for b, k in mp_peers:
        i = b * 8 + k
        send(ps.at[0], ps.at[i], p_s, p_r, on_mp(half_l(b), z + k))

    ln0 = row_of(ln_column[0:128])
    ln1 = row_of(jnp.concatenate([ln_column[128:192], jnp.zeros((64, 1), F32)], axis=0))
    ga[0] = jnp.concatenate([gqg, gkg, ln0, ln1, jnp.zeros((4, 128), F32)], axis=0)
    quad = (on_dp(y, h, 1 - c), on_dp(y, 1 - h, c), on_dp(y, 1 - h, 1 - c))
    for i, p in enumerate(quad):
        send(ga.at[0], ga.at[i + 1], g_s.at[0], g_r.at[0], p)

    def out_block(yy, hh):
        rows = pl.ds(pl.multiple_of(c * 128 + hh * 64, 64), 64)
        return gwo_ref.at[rows, pl.ds(pl.multiple_of(wrap(yy) * 384, 128), 384)]

    def blk_out(off, b):
        return out_block(y + off, half_h(b))

    out_block(y, h)[...] = ((out_sum + ring_out.partner()) * FACTOR).astype(BF16)
    ga_ring = Gather(blk_out, a_s, a_r, y_near, forward=(ac_s, ac_r))
    ga_ring.start()

    in_sum = ring_in.finish()
    ga_ring.start_partner()

    wait_bytes(ga.at[1:4], g_r.at[0])
    gb[0] = (ga[0] + ga[1]) + (ga[2] + ga[3])
    for k in range(1, RING):
        send(gb.at[0], gb.at[k], g_s.at[1], g_r.at[1], on_dp(y + k, h, c))

    step_rings((ga_ring,), 1)

    acc = ps[0]
    wait_bytes(ps.at[1:16], p_r)
    for i in range(1, 16):
        acc = acc + ps[i]
    mean0, mean1 = acc[0:1] * (1.0 / WIDTH), acc[1:2] * (1.0 / WIDTH)
    cot_own = xg[mp, 192:384, :].astype(F32)
    gx_ref[...] = (cot_own + x_inv * (scaled - mean0 - hat * mean1)).astype(BF16)

    step_rings((ga_ring,), 2)
    gwi_ref[...] = ((in_sum + ring_in.partner()) * FACTOR).astype(BF16)
    step_rings((ga_ring,), 3)
    total = gb[0]
    wait_bytes(gb.at[1:8], g_r.at[1])
    for k in range(1, RING):
        total = total + gb[k]
    gs_ref[...] = total * FACTOR
    step_rings((ga_ring,), 4)
    wait_bytes(out_snd.at[0:16], ac_r)

    for ref, sem in (
        (xg.at[0:15], x_s), (wf.at[0:15], w_s), (wf.at[0:16], wc_s),
        (dys, sb_s.at[0]), (jt.at[1], sb_s.at[1]), (gp2.at[0], sb_s.at[2]), (xts, sb_s.at[3]),
        (in_snd.at[0:15], i_s), (out_snd.at[0:15], o_s), (out_snd.at[0:15], a_s), (out_snd.at[0:16], ac_s),
        (dxt.at[0:15], d_s), (ps.at[0:15], p_s), (ga.at[0:3], g_s.at[0]), (gb.at[0:7], g_s.at[1]),
    ):
        wait_bytes(ref, sem)


def per_device(activations, cotangent, ln_gain, w_in, w_out, q_gain, k_gain):
    hbm = pl.BlockSpec(memory_space=pltpu.HBM)
    vmem = pl.BlockSpec(memory_space=pltpu.VMEM)
    dma = pltpu.SemaphoreType.DMA

    def buf(*shape, dtype=BF16):
        return pltpu.VMEM(shape, dtype)

    scratch = [
        buf(192), buf(256, 3072), buf(1, 128), buf(1, 128),
        buf(32, 96, 512),
        buf(16, 400, 128),
        buf(16, 2, 96, 128), buf(16, 96, 128),
        buf(16, 192, 128),
        buf(16, 64, 384, dtype=F32),
        buf(3, 128, 128),
        buf(2, 128, 512),
        buf(16, 96, 512), buf(16, 96, 512), buf(16, 64, 384), buf(16, 64, 384),
        buf(16, 192, 128), buf(16, 192, 128),
        buf(16, 8, 128, dtype=F32), buf(4, 8, 128, dtype=F32), buf(8, 8, 128, dtype=F32),
        dma((7,)), dma, dma((16,)), dma, dma, dma, dma((16,)), dma((4,)), dma((4,)),
        dma, dma((16,)), dma, dma((16,)), dma, dma((16,)), dma, dma,
        dma, dma, dma, dma, dma((2,)), dma((2,)),
    ]
    args = (activations.T, cotangent.T, ln_gain, w_in, w_out, q_gain, k_gain)
    grad_x, grad_w_in, grad_w_out, sums = pl.pallas_call(
        kernel,
        out_shape=(
            jax.ShapeDtypeStruct((192, 128), BF16),
            jax.ShapeDtypeStruct((96, 512), BF16),
            jax.ShapeDtypeStruct((256, 3072), BF16),
            jax.ShapeDtypeStruct((8, 128), F32),
        ),
        in_specs=[hbm] * 7,
        out_specs=(vmem,) * 4,
        scratch_shapes=scratch,
        compiler_params=pltpu.CompilerParams(collective_id=0, has_side_effects=True, vmem_limit_bytes=48 << 20),
    )(*(pltpu.with_memory_space_constraint(a, pltpu.HBM) for a in args))
    grad_ln = jnp.concatenate([sums[2], sums[3, 0:64]])
    return grad_x.T, grad_w_in, grad_w_out, grad_ln, sums[0:1], sums[1:2]


def solution(mesh):
    in_specs = (P("dp", "mp"), P("dp", "mp"), P("mp"), P("dp", "mp"), P("mp", None), P("mp", None), P("mp", None))
    out_specs = (P("dp", "mp"), P("dp", "mp"), P("mp", None), P("mp"), P("mp", None), P("mp", None))
    return jax.shard_map(per_device, mesh=mesh, in_specs=in_specs, out_specs=out_specs, check_vma=False)
```

```python
import jax
import jax.numpy as jnp
from jax import lax
from jax.experimental import pallas as pl
from jax.experimental.pallas import tpu as pltpu
from jax.sharding import PartitionSpec as P

F32 = jnp.float32
BF16 = jnp.bfloat16
EPS = 1e-6
RING = 8
WIDTH = 3072
FACTOR = 1.0 / 32.0


def dot(a, b):
    return jnp.dot(a, b, preferred_element_type=F32)


def dot_t(a, b):
    return lax.dot_general(a, b, (((1,), (1,)), ((), ())), preferred_element_type=F32)


def normalize(v):
    mean = jnp.mean(v, axis=-1, keepdims=True)
    cen = v - mean
    inv = lax.rsqrt(jnp.mean(cen * cen, axis=-1, keepdims=True) + EPS)
    return cen * inv, inv


def norm_back(u, hat, inv):
    m0 = jnp.mean(u, axis=-1, keepdims=True)
    m1 = jnp.mean(u * hat, axis=-1, keepdims=True)
    return inv * (u - m0 - hat * m1)


def rows8(v):
    return jnp.sum(v.reshape(v.shape[0] // 8, 8, 128), axis=0)


def row_of(column):
    return jnp.broadcast_to(column, (128, 128)).T[0:1]


def column_of(row):
    return jnp.broadcast_to(row, (128, 128)).T


def chain_len(d, b):
    return 4 if d == b else 3


def slot(d, b, s):
    return d * 8 + b * 4 + s


def kernel(
    act_h, cot_h, gain_h, win_h, wout_h, qg_h, kg_h,
    gx_ref, gwi_ref, gwo_ref, gs_ref,
    gain_v, wout, qg_v, kg_v,
    wf, xg, xt, xts, dys, ot, jt, gp2,
    in_snd, in_rcv, out_x, out_snd, out_rcv, dxt, dxr, ps, ga, gb,
    ld, w_s, w_r, wc_s, wc_r, x_s, x_r, sb_s, sb_r,
    i_s, i_r, ox_s, ox_r, o_s, o_r, a_s, a_r, ax_s, ax_r, ac_s, ac_r, d_s, d_r, p_s, p_r, g_s, g_r,
):
    dp = lax.axis_index("dp")
    mp = lax.axis_index("mp")
    y, h, c = dp // 4, (dp // 2) % 2, dp % 2
    l, z = mp // RING, mp % RING

    def wrap(i):
        return lax.rem(i + 2 * RING, RING)

    def dpi(yy, hh, cc):
        return (wrap(yy) * 2 + hh) * 2 + cc

    def mpi(ll, zz):
        return ll * RING + wrap(zz)

    def on_dp(yy, hh, cc):
        return {"dp": dpi(yy, hh, cc), "mp": mp}

    def on_mp(ll, zz):
        return {"dp": dp, "mp": mpi(ll, zz)}

    sibling = on_dp(y, h, 1 - c)

    loads = []
    for i, (src, dst) in enumerate(
        ((gain_h, gain_v), (act_h, xg.at[mp, 0:192]), (cot_h, xg.at[mp, 192:384]), (win_h, wf.at[dp]), (qg_h, qg_v), (kg_h, kg_v), (wout_h, wout))
    ):
        cp = pltpu.make_async_copy(src, dst, ld.at[i])
        cp.start()
        loads.append(cp)

    barrier = pltpu.get_barrier_semaphore()
    peers = [on_dp(y + k, h, c) for k in range(1, RING)]
    peers += [sibling, on_dp(y, 1 - h, c), on_dp(y, 1 - h, 1 - c), on_dp(y + 1, 1 - h, c), on_dp(y - 1, 1 - h, c)]
    peers += [on_mp(l, z + k) for k in range(1, RING)] + [on_mp(1 - l, z + k) for k in range(RING)]
    for p in peers:
        pl.semaphore_signal(barrier, inc=1, device_id=p, device_id_type=pl.DeviceIdType.MESH)

    loads[0].wait()
    gain = gain_v[...].astype(F32).reshape(1, 192)
    gain0 = gain[:, 0:128]
    gain1 = jnp.concatenate([gain[:, 128:192], gain[:, 128:192]], axis=1)
    xg[mp, 384:400, :] = jnp.concatenate(
        [jnp.broadcast_to(gain0, (8, 128)), jnp.broadcast_to(gain1, (8, 128))], axis=0
    ).astype(BF16)
    for i in range(1, 4):
        loads[i].wait()
    pl.semaphore_wait(barrier, len(peers))

    def remote(src, dst, snd, rcv, to):
        return pltpu.make_async_remote_copy(
            src_ref=src, dst_ref=dst, send_sem=snd, recv_sem=rcv, device_id=to, device_id_type=pl.DeviceIdType.MESH
        )

    def send(src, dst, snd, rcv, to):
        remote(src, dst, snd, rcv, to).start()

    def wait_bytes(ref, sem):
        pltpu.make_async_copy(ref, ref, sem).wait()

    class Gather:
        def __init__(self, blk, snd, rcv, near, forward=None):
            self.blk, self.snd, self.rcv = blk, snd, rcv
            self.near, self.pair, self.forward = near[0:2], near[2], forward

        def _fwd(self, off, b):
            if self.forward is not None:
                s, r = self.forward
                ref = self.blk(off, b)
                send(ref, ref, s, r, sibling)

        def _send(self, off, b, i, to):
            ref = self.blk(off, b)
            send(ref, ref, self.snd, self.rcv.at[i], to)

        def start(self):
            self._send(0, 0, 7, self.pair)
            for d in range(2):
                self._send(0, 0, slot(d, 0, 0), self.near[d])
            self._fwd(0, 0)

        def start_partner(self):
            self.arrive(0, 1, 7, self.pair)
            for d in range(2):
                self._send(0, 1, slot(d, 1, 0), self.near[d])
            self._fwd(0, 1)

        def arrive(self, off, b, i, to):
            ref = self.blk(off, b)
            remote(ref, ref, self.snd, self.rcv.at[i], to).wait_recv()

        def step(self, st, b):
            for d in range(2):
                n = chain_len(d, b)
                if st > n:
                    continue
                off = -st if d == 0 else st
                self.arrive(off, b, slot(d, b, st - 1), self.near[d])
                if st < n:
                    self._send(off, b, slot(d, b, st), self.near[d])
                self._fwd(off, b)

    def start_rings(rings):
        for r in rings:
            r.start()
        for r in rings:
            r.start_partner()

    def step_rings(rings, st):
        for b in range(2):
            for r in rings:
                r.step(st, b)

    def half_h(b):
        return h if b == 0 else 1 - h

    def half_l(b):
        return l if b == 0 else 1 - l

    y_near = (on_dp(y + 1, h, c), on_dp(y - 1, h, c), on_dp(y, 1 - h, c))
    z_near = (on_mp(l, z + 1), on_mp(l, z - 1), on_mp(1 - l, z))
    gx_ring = Gather(lambda off, b: xg.at[mpi(half_l(b), z + off)], x_s, x_r, z_near)
    gw_ring = Gather(lambda off, b: wf.at[dpi(y + off, half_h(b), c)], w_s, w_r, y_near, forward=(wc_s, wc_r))
    start_rings((gx_ring, gw_ring))

    for i in range(4, 7):
        loads[i].wait()

    def process(q, carry):
        gcat, sums = carry
        for b in range(2):
            j = half_l(b) * 4 + lax.rem(z // 2 + q + 4, 4)
            pair = xg[pl.ds(2 * j, 2)]
            sums = sums + rows8(pair[:, 0:192].reshape(384, 128).astype(F32))
            dy = pair[:, 192:384].reshape(384, 128)
            gcat = gcat + dot(wout[:, pl.ds(pl.multiple_of(j * 384, 128), 384)], dy)
        return gcat, sums

    carry = (jnp.zeros((256, 128), F32), jnp.zeros((8, 128), F32))
    for st in range(1, 5):
        step_rings((gx_ring, gw_ring), st)
        if st == 1:
            carry = process(0, carry)
        if st == 3:
            carry = process(1, carry)
            carry = process(-1, carry)
        if st == 4:
            carry = process(2, carry)
    grad_cat, sums = carry
    send(xg.at[:, 192:384], dys, sb_s.at[0], sb_r.at[0], sibling)

    x_mean = jnp.sum(sums, axis=0, keepdims=True) * (1.0 / WIDTH)

    def var_body(m, acc):
        v = xg[m, 0:192, :].astype(F32) - x_mean
        return acc + rows8(v * v)

    var = lax.fori_loop(0, 16, var_body, jnp.zeros((8, 128), F32))
    x_inv = lax.rsqrt(jnp.sum(var, axis=0, keepdims=True) * (1.0 / WIDTH) + EPS)

    gain_rows = []
    for m in range(16):
        t = xg[m, 384:400, :].astype(F32)
        gain_rows += [t[0:1], t[8:9]]
    gains = jnp.concatenate(gain_rows + [jnp.zeros((96, 128), F32)], axis=0).T

    wait_bytes(wf.at[0:16], wc_r)

    proj = jnp.zeros((128, 512), F32)
    for j in range(8):
        parts = []
        for m in (2 * j, 2 * j + 1):
            v = (xg[m, 0:192, :].astype(F32) - x_mean) * x_inv
            top = v[0:128] * gains[:, 2 * m : 2 * m + 1]
            bottom = v[128:192] * gains[0:64, 2 * m + 1 : 2 * m + 2]
            parts += [top, bottom]
        v = jnp.concatenate(parts, axis=0)
        xt[2 * j : 2 * j + 2] = v.astype(BF16).reshape(2, 2, 96, 128)
        vt = jnp.concatenate([v[k * 128 : (k + 1) * 128].T for k in range(3)], axis=1).astype(BF16)
        proj = proj + dot(vt, wf[4 * j : 4 * j + 4].reshape(384, 512))
    send(xt.at[:, 1 - c], xts, sb_s.at[3], sb_r.at[3], sibling)

    pre = proj[:, 384:512]
    cdf = 0.5 * (1.0 + lax.erf(pre * 0.7071067811865476))
    pdf = jnp.exp(-0.5 * pre * pre) * 0.3989422804014327
    act = pre * cdf
    grad_pre = grad_cat[128:256].T * (cdf + pre * pdf)

    scaling = 128.0 ** -0.5
    qg, kg = qg_v[...].astype(F32), kg_v[...].astype(F32)
    q_hat, q_inv = normalize(proj[:, 0:128])
    k_hat, k_inv = normalize(proj[:, 128:256])
    qn, kn = (q_hat * qg).astype(BF16), (k_hat * kg).astype(BF16)
    v_bf = proj[:, 256:384].astype(BF16)
    go = grad_cat[0:128].T.astype(BF16)
    sc = dot_t(qn, kn) * scaling
    e = jnp.exp(sc - jnp.max(sc, axis=-1, keepdims=True))
    prob = e / jnp.sum(e, axis=-1, keepdims=True)
    out = dot(prob.astype(BF16), v_bf)

    is0 = jnp.full((128, 128), c, jnp.int32) == 0
    jt[0] = jnp.where(is0, out, act).T.astype(BF16)
    jt[1] = jnp.where(is0, act, out).T.astype(BF16)
    send(jt.at[1], jt.at[2], sb_s.at[1], sb_r.at[1], sibling)

    gprob = dot_t(go, v_bf)
    grad_v = dot(prob.T.astype(BF16), go)
    gsc = prob * (gprob - jnp.sum(prob * gprob, axis=-1, keepdims=True)) * scaling
    gqn = dot(gsc.astype(BF16), kn)
    gkn = dot(gsc.T.astype(BF16), qn)
    gqg = jnp.sum(gqn * q_hat, axis=0, keepdims=True)
    gkg = jnp.sum(gkn * k_hat, axis=0, keepdims=True)
    grad_q = norm_back(gqn * qg, q_hat, q_inv)
    grad_k = norm_back(gkn * kg, k_hat, k_inv)
    gp = jnp.concatenate([grad_q, grad_k, grad_v, grad_pre], axis=1).astype(BF16)
    gp2[0] = gp
    send(gp2.at[0], gp2.at[1], sb_s.at[2], sb_r.at[2], sibling)

    remote(jt.at[1], jt.at[2], sb_s.at[1], sb_r.at[1], sibling).wait_recv()
    remote(xg.at[:, 192:384], dys, sb_s.at[0], sb_r.at[0], sibling).wait_recv()
    jt_cat = jnp.concatenate([jt[0], jt[2]], axis=1)

    def ot_body(j, _):
        own = xg[pl.ds(2 * j, 2), 192:384, :].reshape(384, 128)
        other = dys[pl.ds(2 * j, 2)].reshape(384, 128)
        t = dot_t(jt_cat, jnp.concatenate([own, other], axis=1))
        ot[pl.ds(2 * j, 2)] = t.astype(BF16).reshape(2, 64, 384)
        return 0

    lax.fori_loop(0, 8, ot_body, 0)

    far_first = (4, 3, 5, 2, 6, 1, 7, 0)
    near_first = (1, 7, 2, 6, 3, 5, 4)
    for k in far_first:
        send(ot.at[wrap(y + k) * 2 + 1 - h], out_x.at[k], ox_s, ox_r.at[k], y_near[2])

    def out_pass(ks):
        for k in ks:
            remote(ot.at[0], out_x.at[k], ox_s, ox_r.at[k], y_near[2]).wait_recv()
            value = ot[wrap(y + k) * 2 + h].astype(F32) + out_x[k].astype(F32)
            out_snd[k] = value.astype(BF16)
            if k:
                send(out_snd.at[k], out_rcv.at[k], o_s, o_r, on_dp(y + k, h, c))

    class Reduce:
        def __init__(self, term, snd, rcv, s, r, near):
            self.term, self.snd, self.rcv, self.s, self.r = term, snd, rcv, s, r
            self.near, self.pair = near[0:2], near[2]

        def _send(self, i, value, to):
            self.snd[i] = value.astype(BF16)
            send(self.snd.at[i], self.rcv.at[i], self.s, self.r.at[i], to)

        def arrived(self, i, to):
            remote(self.snd.at[i], self.rcv.at[i], self.s, self.r.at[i], to).wait_recv()
            return self.rcv[i].astype(F32)

        def step(self, st):
            for b in range(2):
                for d in range(2):
                    n = chain_len(d, b)
                    if st >= n:
                        continue
                    off = (n - st) if d == 0 else st - n
                    value = self.term(off, b)
                    if st > 0:
                        value = value + self.arrived(slot(d, b, st - 1), self.near[d])
                    self._send(slot(d, b, st), value, self.near[d])

        def total(self, b):
            value = self.term(0, b)
            for d in range(2):
                value = value + self.arrived(slot(d, b, chain_len(d, b) - 1), self.near[d])
            return value

        def finish(self):
            self._send(7, self.total(1), self.pair)
            return self.total(0)

        def partner(self):
            return self.arrived(7, self.pair)

    def term_in(off, b):
        i = wrap(y + off) * 2 + half_h(b)
        return dot(jnp.concatenate([xt[i, c], xts[i]], axis=1), gp2[...].reshape(256, 512))

    ring_in = Reduce(term_in, in_snd, in_rcv, i_s, i_r, y_near)

    remote(gp2.at[0], gp2.at[1], sb_s.at[2], sb_r.at[2], sibling).wait_recv()
    remote(xt.at[:, 1 - c], xts, sb_s.at[3], sb_r.at[3], sibling).wait_recv()
    ring_in.step(0)

    def dx_body(j, _):
        w = wf[pl.ds(4 * j, 4)].reshape(384, 512)
        dxt[pl.ds(2 * j, 2)] = dot_t(w, gp2[0]).astype(BF16).reshape(2, 192, 128)
        return 0

    lax.fori_loop(0, 8, dx_body, 0)
    mp_peers = [(b, k) for k in (4, 3, 5, 2, 6, 1, 7, 0) for b in range(2) if (b, k) != (0, 0)]
    for b, k in mp_peers:
        i = b * 8 + k
        send(dxt.at[mpi(half_l(b), z + k)], dxr.at[i], d_s, d_r, on_mp(half_l(b), z + k))

    out_pass(far_first[:6])
    ring_in.step(1)
    out_pass(far_first[6:])
    ring_in.step(2)

    def out_block(yy, hh):
        rows = pl.ds(pl.multiple_of(c * 128 + hh * 64, 64), 64)
        return gwo_ref.at[rows, pl.ds(pl.multiple_of(wrap(yy) * 384, 128), 384)]

    def halves(yy):
        cols = pl.ds(pl.multiple_of(wrap(yy) * 384, 128), 384)
        return [gwo_ref.at[pl.ds(pl.multiple_of(c * 128 + h * 64 + 32 * i, 32), 32), cols] for i in range(2)]

    wait_bytes(out_rcv.at[1:8], o_r)
    out_sum = out_snd[0].astype(F32)
    for k in range(1, RING):
        out_sum = out_sum + out_rcv[k].astype(F32)
    own_out = out_block(y, h)
    own_out[...] = (out_sum * FACTOR).astype(BF16)
    for k in (1, 7, 2, 6):
        send(own_out, own_out, a_s, a_r.at[k], on_dp(y + k, h, c))
    send(own_out, own_out, ax_s, ax_r.at[0], y_near[2])
    send(own_out, own_out, ac_s, ac_r, sibling)


    dxn = dxt[mp].astype(F32)
    wait_bytes(dxr.at[1:16], d_r)
    for i in range(1, 16):
        dxn = dxn + dxr[i].astype(F32)

    own_gain = jnp.concatenate([column_of(gain0), column_of(gain1)[0:64]], axis=0)
    hat = (xg[mp, 0:192, :].astype(F32) - x_mean) * x_inv
    ln_column = jnp.sum(dxn * hat, axis=1, keepdims=True)
    scaled = dxn * own_gain
    sum0 = jnp.sum(scaled, axis=0, keepdims=True)
    sum1 = jnp.sum(scaled * hat, axis=0, keepdims=True)
    ps[0] = jnp.concatenate([sum0, sum1, jnp.zeros((6, 128), F32)], axis=0)
    for b, k in mp_peers:
        i = b * 8 + k
        send(ps.at[0], ps.at[i], p_s, p_r, on_mp(half_l(b), z + k))

    ln0 = row_of(ln_column[0:128])
    ln1 = row_of(jnp.concatenate([ln_column[128:192], jnp.zeros((64, 1), F32)], axis=0))
    ga[0] = jnp.concatenate([gqg, gkg, ln0, ln1, jnp.zeros((4, 128), F32)], axis=0)
    quad = (on_dp(y, h, 1 - c), on_dp(y, 1 - h, c), on_dp(y, 1 - h, 1 - c))
    for i, p in enumerate(quad):
        send(ga.at[0], ga.at[i + 1], g_s.at[0], g_r.at[0], p)

    ring_in.step(3)

    wait_bytes(ga.at[1:4], g_r.at[0])
    gb[0] = (ga[0] + ga[1]) + (ga[2] + ga[3])
    for k in range(1, RING):
        send(gb.at[0], gb.at[k], g_s.at[1], g_r.at[1], on_dp(y + k, h, c))

    for k in (1, 7, 2, 6, 3, 5, 4):
        ref = out_block(y - k, h)
        if k == 4:
            for i, part in enumerate(halves(y - k)):
                remote(part, part, a_s, a_r.at[(4, 0)[i]], sibling).wait_recv()
        else:
            remote(ref, ref, a_s, a_r.at[k], sibling).wait_recv()
        if k in (2, 6):
            turn = 1 if k == 2 else -1
            part = halves(y - k)[(2, 6).index(k)]
            send(ref, ref, a_s, a_r.at[k + turn], on_dp(y + turn, h, c))
            send(part, part, a_s, a_r.at[(4, 0)[(2, 6).index(k)]], on_dp(y + 2 * turn, h, c))
        send(ref, ref, ax_s, ax_r.at[k], y_near[2])
        send(ref, ref, ac_s, ac_r, sibling)

    in_sum = ring_in.finish()

    acc = ps[0]
    wait_bytes(ps.at[1:16], p_r)
    for i in range(1, 16):
        acc = acc + ps[i]
    mean0, mean1 = acc[0:1] * (1.0 / WIDTH), acc[1:2] * (1.0 / WIDTH)
    cot_own = xg[mp, 192:384, :].astype(F32)
    gx_ref[...] = (cot_own + x_inv * (scaled - mean0 - hat * mean1)).astype(BF16)

    for k in (0,) + near_first:
        ref = out_block(y - k, 1 - h)
        remote(ref, ref, ax_s, ax_r.at[k], y_near[2]).wait_recv()
        send(ref, ref, ac_s, ac_r, sibling)

    gwi_ref[...] = ((in_sum + ring_in.partner()) * FACTOR).astype(BF16)
    total = gb[0]
    wait_bytes(gb.at[1:8], g_r.at[1])
    for k in range(1, RING):
        total = total + gb[k]
    gs_ref[...] = total * FACTOR
    wait_bytes(ot.at[0:16], ac_r)

    for ref, sem in (
        (xg.at[0:15], x_s), (wf.at[0:15], w_s), (wf.at[0:16], wc_s),
        (dys, sb_s.at[0]), (jt.at[1], sb_s.at[1]), (gp2.at[0], sb_s.at[2]), (xts, sb_s.at[3]),
        (in_snd.at[0:15], i_s), (ot.at[0:8], ox_s), (ot.at[0:7], o_s), (ot.at[0:7], a_s), (ot.at[0:8], ax_s), (ot.at[0:16], ac_s),
        (dxt.at[0:15], d_s), (ps.at[0:15], p_s), (ga.at[0:3], g_s.at[0]), (gb.at[0:7], g_s.at[1]),
    ):
        wait_bytes(ref, sem)


def per_device(activations, cotangent, ln_gain, w_in, w_out, q_gain, k_gain):
    hbm = pl.BlockSpec(memory_space=pltpu.HBM)
    vmem = pl.BlockSpec(memory_space=pltpu.VMEM)
    dma = pltpu.SemaphoreType.DMA

    def buf(*shape, dtype=BF16):
        return pltpu.VMEM(shape, dtype)

    scratch = [
        buf(192), buf(256, 3072), buf(1, 128), buf(1, 128),
        buf(32, 96, 512),
        buf(16, 400, 128),
        buf(16, 2, 96, 128), buf(16, 96, 128),
        buf(16, 192, 128),
        buf(16, 64, 384),
        buf(3, 128, 128),
        buf(2, 128, 512),
        buf(16, 96, 512), buf(16, 96, 512), buf(8, 64, 384), buf(8, 64, 384), buf(8, 64, 384),
        buf(16, 192, 128), buf(16, 192, 128),
        buf(16, 8, 128, dtype=F32), buf(4, 8, 128, dtype=F32), buf(8, 8, 128, dtype=F32),
        dma((7,)), dma, dma((16,)), dma, dma, dma, dma((16,)), dma((4,)), dma((4,)),
        dma, dma((16,)), dma, dma((8,)), dma, dma, dma, dma((8,)), dma, dma((8,)), dma, dma,
        dma, dma, dma, dma, dma((2,)), dma((2,)),
    ]
    args = (activations.T, cotangent.T, ln_gain, w_in, w_out, q_gain, k_gain)
    grad_x, grad_w_in, grad_w_out, sums = pl.pallas_call(
        kernel,
        out_shape=(
            jax.ShapeDtypeStruct((192, 128), BF16),
            jax.ShapeDtypeStruct((96, 512), BF16),
            jax.ShapeDtypeStruct((256, 3072), BF16),
            jax.ShapeDtypeStruct((8, 128), F32),
        ),
        in_specs=[hbm] * 7,
        out_specs=(vmem,) * 4,
        scratch_shapes=scratch,
        compiler_params=pltpu.CompilerParams(collective_id=0, has_side_effects=True, vmem_limit_bytes=48 << 20),
    )(*(pltpu.with_memory_space_constraint(a, pltpu.HBM) for a in args))
    grad_ln = jnp.concatenate([sums[2], sums[3, 0:64]])
    return grad_x.T, grad_w_in, grad_w_out, grad_ln, sums[0:1], sums[1:2]


def solution(mesh):
    in_specs = (P("dp", "mp"), P("dp", "mp"), P("mp"), P("dp", "mp"), P("mp", None), P("mp", None), P("mp", None))
    out_specs = (P("dp", "mp"), P("dp", "mp"), P("mp", None), P("mp"), P("mp", None), P("mp", None))
    return jax.shard_map(per_device, mesh=mesh, in_specs=in_specs, out_specs=out_specs, check_vma=False)
```

```python
import jax
import jax.numpy as jnp
from jax import lax
from jax.experimental import pallas as pl
from jax.experimental.pallas import tpu as pltpu
from jax.sharding import PartitionSpec as P

F32 = jnp.float32
BF16 = jnp.bfloat16
EPS = 1e-6
RING = 8
WIDTH = 3072
FACTOR = 1.0 / 32.0


def dot(a, b):
    return jnp.dot(a, b, preferred_element_type=F32)


def dot_t(a, b):
    return lax.dot_general(a, b, (((1,), (1,)), ((), ())), preferred_element_type=F32)


def normalize(v):
    mean = jnp.mean(v, axis=-1, keepdims=True)
    cen = v - mean
    inv = lax.rsqrt(jnp.mean(cen * cen, axis=-1, keepdims=True) + EPS)
    return cen * inv, inv


def norm_back(u, hat, inv):
    m0 = jnp.mean(u, axis=-1, keepdims=True)
    m1 = jnp.mean(u * hat, axis=-1, keepdims=True)
    return inv * (u - m0 - hat * m1)


def rows8(v):
    return jnp.sum(v.reshape(v.shape[0] // 8, 8, 128), axis=0)


def row_of(column):
    return jnp.broadcast_to(column, (128, 128)).T[0:1]


def column_of(row):
    return jnp.broadcast_to(row, (128, 128)).T


def chain_len(d, b):
    return 4 if d == b else 3


def slot(d, b, s):
    return d * 8 + b * 4 + s


def kernel(
    act_h, cot_h, gain_h, win_h, wout_h, qg_h, kg_h,
    gx_ref, gwi_ref, gwo_ref, gln_ref, gq_ref, gk_ref,
    gain_v, wout, qg_v, kg_v,
    wf, xg, xt, xts, dys, ot, jt, gp2,
    in_snd, in_rcv, out_x, out_snd, out_rcv, dxt, dxr, ps, ga, gb,
    ld, w_s, w_r, wc_s, wc_r, x_s, x_r, sb_s, sb_r,
    i_s, i_r, ox_s, ox_r, o_s, o_r, a_s, a_r, ax_s, ax_r, ac_s, ac_r, d_s, d_r, p_s, p_r, g_s, g_r,
):
    dp = lax.axis_index("dp")
    mp = lax.axis_index("mp")
    y, h, c = dp // 4, (dp // 2) % 2, dp % 2
    l, z = mp // RING, mp % RING

    def wrap(i):
        return lax.rem(i + 2 * RING, RING)

    def dpi(yy, hh, cc):
        return (wrap(yy) * 2 + hh) * 2 + cc

    def mpi(ll, zz):
        return ll * RING + wrap(zz)

    def on_dp(yy, hh, cc):
        return {"dp": dpi(yy, hh, cc), "mp": mp}

    def on_mp(ll, zz):
        return {"dp": dp, "mp": mpi(ll, zz)}

    sibling = on_dp(y, h, 1 - c)

    loads = []
    for i, (src, dst) in enumerate(
        ((gain_h, gain_v), (act_h, xg.at[mp, 0:192]), (cot_h, xg.at[mp, 192:384]), (win_h, wf.at[dp]), (qg_h, qg_v), (kg_h, kg_v), (wout_h, wout))
    ):
        cp = pltpu.make_async_copy(src, dst, ld.at[i])
        cp.start()
        loads.append(cp)

    barrier = pltpu.get_barrier_semaphore()
    peers = [on_dp(y + k, h, c) for k in range(1, RING)]
    peers += [sibling, on_dp(y, 1 - h, c), on_dp(y, 1 - h, 1 - c), on_dp(y + 1, 1 - h, c), on_dp(y - 1, 1 - h, c)]
    peers += [on_mp(l, z + k) for k in range(1, RING)] + [on_mp(1 - l, z + k) for k in range(RING)]
    for p in peers:
        pl.semaphore_signal(barrier, inc=1, device_id=p, device_id_type=pl.DeviceIdType.MESH)

    loads[0].wait()
    gain = gain_v[...].astype(F32).reshape(1, 192)
    gain0 = gain[:, 0:128]
    gain1 = jnp.concatenate([gain[:, 128:192], gain[:, 128:192]], axis=1)
    xg[mp, 384:400, :] = jnp.concatenate(
        [jnp.broadcast_to(gain0, (8, 128)), jnp.broadcast_to(gain1, (8, 128))], axis=0
    ).astype(BF16)
    for i in range(1, 4):
        loads[i].wait()
    pl.semaphore_wait(barrier, len(peers))

    def remote(src, dst, snd, rcv, to):
        return pltpu.make_async_remote_copy(
            src_ref=src, dst_ref=dst, send_sem=snd, recv_sem=rcv, device_id=to, device_id_type=pl.DeviceIdType.MESH
        )

    def send(src, dst, snd, rcv, to):
        remote(src, dst, snd, rcv, to).start()

    def wait_bytes(ref, sem):
        pltpu.make_async_copy(ref, ref, sem).wait()

    class Gather:
        def __init__(self, blk, snd, rcv, near, forward=None):
            self.blk, self.snd, self.rcv = blk, snd, rcv
            self.near, self.pair, self.forward = near[0:2], near[2], forward

        def _fwd(self, off, b):
            if self.forward is not None:
                s, r = self.forward
                ref = self.blk(off, b)
                send(ref, ref, s, r, sibling)

        def _send(self, off, b, i, to):
            ref = self.blk(off, b)
            send(ref, ref, self.snd, self.rcv.at[i], to)

        def start(self):
            self._send(0, 0, 7, self.pair)
            for d in range(2):
                self._send(0, 0, slot(d, 0, 0), self.near[d])
            self._fwd(0, 0)

        def start_partner(self):
            self.arrive(0, 1, 7, self.pair)
            for d in range(2):
                self._send(0, 1, slot(d, 1, 0), self.near[d])
            self._fwd(0, 1)

        def arrive(self, off, b, i, to):
            ref = self.blk(off, b)
            remote(ref, ref, self.snd, self.rcv.at[i], to).wait_recv()

        def step(self, st, b):
            for d in range(2):
                n = chain_len(d, b)
                if st > n:
                    continue
                off = -st if d == 0 else st
                self.arrive(off, b, slot(d, b, st - 1), self.near[d])
                if st < n:
                    self._send(off, b, slot(d, b, st), self.near[d])
                self._fwd(off, b)

    def start_rings(rings):
        for r in rings:
            r.start()
        for r in rings:
            r.start_partner()

    def step_rings(rings, st):
        for b in range(2):
            for r in rings:
                r.step(st, b)

    def half_h(b):
        return h if b == 0 else 1 - h

    def half_l(b):
        return l if b == 0 else 1 - l

    y_near = (on_dp(y + 1, h, c), on_dp(y - 1, h, c), on_dp(y, 1 - h, c))
    z_near = (on_mp(l, z + 1), on_mp(l, z - 1), on_mp(1 - l, z))
    gx_ring = Gather(lambda off, b: xg.at[mpi(half_l(b), z + off)], x_s, x_r, z_near)
    gw_ring = Gather(lambda off, b: wf.at[dpi(y + off, half_h(b), c)], w_s, w_r, y_near, forward=(wc_s, wc_r))
    start_rings((gx_ring, gw_ring))

    for i in range(4, 7):
        loads[i].wait()

    def process(q, carry):
        gcat, sums = carry
        for b in range(2):
            j = half_l(b) * 4 + lax.rem(z // 2 + q + 4, 4)
            pair = xg[pl.ds(2 * j, 2)]
            sums = sums + rows8(pair[:, 0:192].reshape(384, 128).astype(F32))
            dy = pair[:, 192:384].reshape(384, 128)
            gcat = gcat + dot(wout[:, pl.ds(pl.multiple_of(j * 384, 128), 384)], dy)
        return gcat, sums

    carry = (jnp.zeros((256, 128), F32), jnp.zeros((8, 128), F32))
    for st in range(1, 5):
        step_rings((gx_ring, gw_ring), st)
        if st == 1:
            carry = process(0, carry)
        if st == 3:
            carry = process(1, carry)
            carry = process(-1, carry)
        if st == 4:
            carry = process(2, carry)
    grad_cat, sums = carry
    send(xg.at[:, 192:384], dys, sb_s.at[0], sb_r.at[0], sibling)

    x_mean = jnp.sum(sums, axis=0, keepdims=True) * (1.0 / WIDTH)

    def var_body(m, acc):
        v = xg[m, 0:192, :].astype(F32) - x_mean
        return acc + rows8(v * v)

    var = lax.fori_loop(0, 16, var_body, jnp.zeros((8, 128), F32))
    x_inv = lax.rsqrt(jnp.sum(var, axis=0, keepdims=True) * (1.0 / WIDTH) + EPS)

    gain_rows = []
    for m in range(16):
        t = xg[m, 384:400, :].astype(F32)
        gain_rows += [t[0:1], t[8:9]]
    gains = jnp.concatenate(gain_rows + [jnp.zeros((96, 128), F32)], axis=0).T

    wait_bytes(wf.at[0:16], wc_r)

    proj = jnp.zeros((128, 512), F32)
    for j in range(8):
        parts = []
        for m in (2 * j, 2 * j + 1):
            v = (xg[m, 0:192, :].astype(F32) - x_mean) * x_inv
            top = v[0:128] * gains[:, 2 * m : 2 * m + 1]
            bottom = v[128:192] * gains[0:64, 2 * m + 1 : 2 * m + 2]
            parts += [top, bottom]
        v = jnp.concatenate(parts, axis=0)
        xt[2 * j : 2 * j + 2] = v.astype(BF16).reshape(2, 2, 96, 128)
        vt = jnp.concatenate([v[k * 128 : (k + 1) * 128].T for k in range(3)], axis=1).astype(BF16)
        proj = proj + dot(vt, wf[4 * j : 4 * j + 4].reshape(384, 512))
    send(xt.at[:, 1 - c], xts, sb_s.at[3], sb_r.at[3], sibling)

    pre = proj[:, 384:512]
    cdf = 0.5 * (1.0 + lax.erf(pre * 0.7071067811865476))
    pdf = jnp.exp(-0.5 * pre * pre) * 0.3989422804014327
    act = pre * cdf
    grad_pre = grad_cat[128:256].T * (cdf + pre * pdf)

    scaling = 128.0 ** -0.5
    qg, kg = qg_v[...].astype(F32), kg_v[...].astype(F32)
    q_hat, q_inv = normalize(proj[:, 0:128])
    k_hat, k_inv = normalize(proj[:, 128:256])
    qn, kn = (q_hat * qg).astype(BF16), (k_hat * kg).astype(BF16)
    v_bf = proj[:, 256:384].astype(BF16)
    go = grad_cat[0:128].T.astype(BF16)
    sc = dot_t(qn, kn) * scaling
    e = jnp.exp(sc - jnp.max(sc, axis=-1, keepdims=True))
    prob = e / jnp.sum(e, axis=-1, keepdims=True)
    out = dot(prob.astype(BF16), v_bf)

    is0 = jnp.full((128, 128), c, jnp.int32) == 0
    jt[0] = jnp.where(is0, out, act).T.astype(BF16)
    jt[1] = jnp.where(is0, act, out).T.astype(BF16)
    send(jt.at[1], jt.at[2], sb_s.at[1], sb_r.at[1], sibling)

    gprob = dot_t(go, v_bf)
    grad_v = dot(prob.T.astype(BF16), go)
    gsc = prob * (gprob - jnp.sum(prob * gprob, axis=-1, keepdims=True)) * scaling
    gqn = dot(gsc.astype(BF16), kn)
    gkn = dot(gsc.T.astype(BF16), qn)
    gqg = jnp.sum(gqn * q_hat, axis=0, keepdims=True)
    gkg = jnp.sum(gkn * k_hat, axis=0, keepdims=True)
    grad_q = norm_back(gqn * qg, q_hat, q_inv)
    grad_k = norm_back(gkn * kg, k_hat, k_inv)
    gp = jnp.concatenate([grad_q, grad_k, grad_v, grad_pre], axis=1).astype(BF16)
    gp2[0] = gp
    send(gp2.at[0], gp2.at[1], sb_s.at[2], sb_r.at[2], sibling)

    remote(jt.at[1], jt.at[2], sb_s.at[1], sb_r.at[1], sibling).wait_recv()
    remote(xg.at[:, 192:384], dys, sb_s.at[0], sb_r.at[0], sibling).wait_recv()
    jt_cat = jnp.concatenate([jt[0], jt[2]], axis=1)

    def ot_body(j, _):
        own = xg[pl.ds(2 * j, 2), 192:384, :].reshape(384, 128)
        other = dys[pl.ds(2 * j, 2)].reshape(384, 128)
        t = dot_t(jt_cat, jnp.concatenate([own, other], axis=1))
        ot[pl.ds(2 * j, 2)] = t.astype(BF16).reshape(2, 64, 384)
        return 0

    lax.fori_loop(0, 8, ot_body, 0)

    far_first = (4, 3, 5, 2, 6, 1, 7, 0)
    near_first = (1, 7, 2, 6, 3, 5, 4)
    for k in far_first:
        send(ot.at[wrap(y + k) * 2 + 1 - h], out_x.at[k], ox_s, ox_r.at[k], y_near[2])

    def out_pass(ks):
        for k in ks:
            remote(ot.at[0], out_x.at[k], ox_s, ox_r.at[k], y_near[2]).wait_recv()
            value = ot[wrap(y + k) * 2 + h].astype(F32) + out_x[k].astype(F32)
            out_snd[k] = value.astype(BF16)
            if k:
                send(out_snd.at[k], out_rcv.at[k], o_s, o_r, on_dp(y + k, h, c))

    class Reduce:
        def __init__(self, term, snd, rcv, s, r, near):
            self.term, self.snd, self.rcv, self.s, self.r = term, snd, rcv, s, r
            self.near, self.pair = near[0:2], near[2]

        def _send(self, i, value, to):
            self.snd[i] = value.astype(BF16)
            send(self.snd.at[i], self.rcv.at[i], self.s, self.r.at[i], to)

        def arrived(self, i, to):
            remote(self.snd.at[i], self.rcv.at[i], self.s, self.r.at[i], to).wait_recv()
            return self.rcv[i].astype(F32)

        def step(self, st):
            for b in range(2):
                for d in range(2):
                    n = chain_len(d, b)
                    if st >= n:
                        continue
                    off = (n - st) if d == 0 else st - n
                    value = self.term(off, b)
                    if st > 0:
                        value = value + self.arrived(slot(d, b, st - 1), self.near[d])
                    self._send(slot(d, b, st), value, self.near[d])

        def total(self, b):
            value = self.term(0, b)
            for d in range(2):
                value = value + self.arrived(slot(d, b, chain_len(d, b) - 1), self.near[d])
            return value

        def finish(self):
            self._send(7, self.total(1), self.pair)
            return self.total(0)

        def partner(self):
            return self.arrived(7, self.pair)

    def term_in(off, b):
        i = wrap(y + off) * 2 + half_h(b)
        return dot(jnp.concatenate([xt[i, c], xts[i]], axis=1), gp2[...].reshape(256, 512))

    ring_in = Reduce(term_in, in_snd, in_rcv, i_s, i_r, y_near)

    remote(gp2.at[0], gp2.at[1], sb_s.at[2], sb_r.at[2], sibling).wait_recv()
    remote(xt.at[:, 1 - c], xts, sb_s.at[3], sb_r.at[3], sibling).wait_recv()
    ring_in.step(0)

    def dx_body(j, _):
        w = wf[pl.ds(4 * j, 4)].reshape(384, 512)
        dxt[pl.ds(2 * j, 2)] = dot_t(w, gp2[0]).astype(BF16).reshape(2, 192, 128)
        return 0

    lax.fori_loop(0, 8, dx_body, 0)
    mp_peers = [(b, k) for k in (4, 3, 5, 2, 6, 1, 7, 0) for b in range(2) if (b, k) != (0, 0)]
    for b, k in mp_peers:
        i = b * 8 + k
        send(dxt.at[mpi(half_l(b), z + k)], dxr.at[i], d_s, d_r, on_mp(half_l(b), z + k))

    out_pass(far_first[:6])
    ring_in.step(1)
    out_pass(far_first[6:])
    ring_in.step(2)

    def out_block(yy, hh):
        rows = pl.ds(pl.multiple_of(c * 128 + hh * 64, 64), 64)
        return gwo_ref.at[rows, pl.ds(pl.multiple_of(wrap(yy) * 384, 128), 384)]

    def halves(yy):
        cols = pl.ds(pl.multiple_of(wrap(yy) * 384, 128), 384)
        return [gwo_ref.at[pl.ds(pl.multiple_of(c * 128 + h * 64 + 32 * i, 32), 32), cols] for i in range(2)]

    wait_bytes(out_rcv.at[1:8], o_r)
    out_sum = out_snd[0].astype(F32)
    for k in range(1, RING):
        out_sum = out_sum + out_rcv[k].astype(F32)
    own_out = out_block(y, h)
    own_out[...] = (out_sum * FACTOR).astype(BF16)
    for k in (1, 7, 2, 6):
        send(own_out, own_out, a_s, a_r.at[k], on_dp(y + k, h, c))
    send(own_out, own_out, ax_s, ax_r.at[0], y_near[2])
    send(own_out, own_out, ac_s, ac_r, sibling)


    dxn = dxt[mp].astype(F32)
    wait_bytes(dxr.at[1:16], d_r)
    for i in range(1, 16):
        dxn = dxn + dxr[i].astype(F32)

    own_gain = jnp.concatenate([column_of(gain0), column_of(gain1)[0:64]], axis=0)
    hat = (xg[mp, 0:192, :].astype(F32) - x_mean) * x_inv
    ln_column = jnp.sum(dxn * hat, axis=1, keepdims=True)
    scaled = dxn * own_gain
    sum0 = jnp.sum(scaled, axis=0, keepdims=True)
    sum1 = jnp.sum(scaled * hat, axis=0, keepdims=True)
    ps[0] = jnp.concatenate([sum0, sum1, jnp.zeros((6, 128), F32)], axis=0)
    for b, k in mp_peers:
        i = b * 8 + k
        send(ps.at[0], ps.at[i], p_s, p_r, on_mp(half_l(b), z + k))

    ln0 = row_of(ln_column[0:128])
    ln1 = row_of(jnp.concatenate([ln_column[128:192], jnp.zeros((64, 1), F32)], axis=0))
    ga[0] = jnp.concatenate([gqg, gkg, ln0, ln1, jnp.zeros((4, 128), F32)], axis=0)
    quad = (on_dp(y, h, 1 - c), on_dp(y, 1 - h, c), on_dp(y, 1 - h, 1 - c))
    for i, p in enumerate(quad):
        send(ga.at[0], ga.at[i + 1], g_s.at[0], g_r.at[0], p)

    ring_in.step(3)

    wait_bytes(ga.at[1:4], g_r.at[0])
    gb[0] = (ga[0] + ga[1]) + (ga[2] + ga[3])
    for k in range(1, RING):
        send(gb.at[0], gb.at[k], g_s.at[1], g_r.at[1], on_dp(y + k, h, c))

    for k in (1, 7, 2, 6, 3, 5, 4):
        ref = out_block(y - k, h)
        if k == 4:
            for i, part in enumerate(halves(y - k)):
                remote(part, part, a_s, a_r.at[(4, 0)[i]], sibling).wait_recv()
        else:
            remote(ref, ref, a_s, a_r.at[k], sibling).wait_recv()
        if k in (2, 6):
            turn = 1 if k == 2 else -1
            part = halves(y - k)[(2, 6).index(k)]
            send(ref, ref, a_s, a_r.at[k + turn], on_dp(y + turn, h, c))
            send(part, part, a_s, a_r.at[(4, 0)[(2, 6).index(k)]], on_dp(y + 2 * turn, h, c))
        send(ref, ref, ax_s, ax_r.at[k], y_near[2])
        send(ref, ref, ac_s, ac_r, sibling)

    in_sum = ring_in.finish()

    acc = ps[0]
    wait_bytes(ps.at[1:16], p_r)
    for i in range(1, 16):
        acc = acc + ps[i]
    mean0, mean1 = acc[0:1] * (1.0 / WIDTH), acc[1:2] * (1.0 / WIDTH)
    cot_own = xg[mp, 192:384, :].astype(F32)
    gx_ref[...] = (cot_own + x_inv * (scaled - mean0 - hat * mean1)).astype(BF16)

    for k in (0,) + near_first:
        ref = out_block(y - k, 1 - h)
        remote(ref, ref, ax_s, ax_r.at[k], y_near[2]).wait_recv()
        send(ref, ref, ac_s, ac_r, sibling)

    gwi_ref[...] = ((in_sum + ring_in.partner()) * FACTOR).astype(BF16)
    total = gb[0]
    wait_bytes(gb.at[1:8], g_r.at[1])
    for k in range(1, RING):
        total = total + gb[k]
    total = total * FACTOR
    gln_ref[...] = jnp.concatenate([total[2:3], total[3:4, 0:64]], axis=1).reshape(192)
    gq_ref[...] = total[0:1]
    gk_ref[...] = total[1:2]
    wait_bytes(ot.at[0:16], ac_r)

    for ref, sem in (
        (xg.at[0:15], x_s), (wf.at[0:15], w_s), (wf.at[0:16], wc_s),
        (dys, sb_s.at[0]), (jt.at[1], sb_s.at[1]), (gp2.at[0], sb_s.at[2]), (xts, sb_s.at[3]),
        (in_snd.at[0:15], i_s), (ot.at[0:8], ox_s), (ot.at[0:7], o_s), (ot.at[0:7], a_s), (ot.at[0:8], ax_s), (ot.at[0:16], ac_s),
        (dxt.at[0:15], d_s), (ps.at[0:15], p_s), (ga.at[0:3], g_s.at[0]), (gb.at[0:7], g_s.at[1]),
    ):
        wait_bytes(ref, sem)


def store(*refs):
    sources, results, sem = refs[0:6], refs[6:12], refs[12]
    copies = [pltpu.make_async_copy(a, b, sem.at[i]) for i, (a, b) in enumerate(zip(sources, results))]
    for cp in copies:
        cp.start()
    for cp in copies:
        cp.wait()


def per_device(activations, cotangent, ln_gain, w_in, w_out, q_gain, k_gain):
    hbm = pl.BlockSpec(memory_space=pltpu.HBM)
    vmem = pl.BlockSpec(memory_space=pltpu.VMEM)
    dma = pltpu.SemaphoreType.DMA

    def buf(*shape, dtype=BF16):
        return pltpu.VMEM(shape, dtype)

    scratch = [
        buf(192), buf(256, 3072), buf(1, 128), buf(1, 128),
        buf(32, 96, 512),
        buf(16, 400, 128),
        buf(16, 2, 96, 128), buf(16, 96, 128),
        buf(16, 192, 128),
        buf(16, 64, 384),
        buf(3, 128, 128),
        buf(2, 128, 512),
        buf(16, 96, 512), buf(16, 96, 512), buf(8, 64, 384), buf(8, 64, 384), buf(8, 64, 384),
        buf(16, 192, 128), buf(16, 192, 128),
        buf(16, 8, 128, dtype=F32), buf(4, 8, 128, dtype=F32), buf(8, 8, 128, dtype=F32),
        dma((7,)), dma, dma((16,)), dma, dma, dma, dma((16,)), dma((4,)), dma((4,)),
        dma, dma((16,)), dma, dma((8,)), dma, dma, dma, dma((8,)), dma, dma((8,)), dma, dma,
        dma, dma, dma, dma, dma((2,)), dma((2,)),
    ]
    args = (activations.T, cotangent.T, ln_gain, w_in, w_out, q_gain, k_gain)
    shapes = (
        jax.ShapeDtypeStruct((192, 128), BF16),
        jax.ShapeDtypeStruct((96, 512), BF16),
        jax.ShapeDtypeStruct((256, 3072), BF16),
        jax.ShapeDtypeStruct((192,), F32),
        jax.ShapeDtypeStruct((1, 128), F32),
        jax.ShapeDtypeStruct((1, 128), F32),
    )
    results = pl.pallas_call(
        kernel,
        out_shape=shapes,
        in_specs=[hbm] * 7,
        out_specs=(vmem,) * 6,
        scratch_shapes=scratch,
        compiler_params=pltpu.CompilerParams(collective_id=0, has_side_effects=True, vmem_limit_bytes=48 << 20),
    )(*(pltpu.with_memory_space_constraint(a, pltpu.HBM) for a in args))
    grad_x, grad_w_in, grad_w_out, grad_ln, grad_q, grad_k = pl.pallas_call(
        store,
        out_shape=shapes,
        in_specs=[pl.BlockSpec(memory_space=pl.ANY)] * 6,
        out_specs=(hbm,) * 6,
        scratch_shapes=[dma((6,))],
        compiler_params=pltpu.CompilerParams(vmem_limit_bytes=1 << 20),
    )(*results)
    return grad_x.T, grad_w_in, grad_w_out, grad_ln, grad_q, grad_k


def solution(mesh):
    in_specs = (P("dp", "mp"), P("dp", "mp"), P("mp"), P("dp", "mp"), P("mp", None), P("mp", None), P("mp", None))
    out_specs = (P("dp", "mp"), P("dp", "mp"), P("mp", None), P("mp"), P("mp", None), P("mp", None))
    return jax.shard_map(per_device, mesh=mesh, in_specs=in_specs, out_specs=out_specs, check_vma=False)
```
